512 devices in a mesh: col: 8 (over x, core), row: 64 (over z, y).
Axes of the slice: x: 4, y: 8, z: 8, core: 2. Of those that a mesh axis runs over, the one named last changes fastest.
Arguments:
- weight_delta: bfloat16 [7168, 32768], P('col', 'row'), may hold values from -96 to 96, as said below
Outputs:
- orthogonalized: bfloat16 [7168, 32768], P('col', 'row')
The draws below stay inside these ranges and needn't reach their ends.
Inputs may be any that keep to these rules, and one draw needn't show every extreme that they name: `weight_delta`: every entry is finite.
All inputs are finite; a program needn't handle non-finite values. Where the reference program divides by a largest or mean magnitude, that divisor is 1e-20 or more.
Results may differ from the reference program's by a relative error of at most 0.0012.
The reference program's roundings to bfloat16 on the way (of `current`, `stacked` and `turning`) count: a program that leaves them out, or rounds other values in their place, can miss the bound.
Values may be sent and summed in bfloat16 or wider, within the bound.
A program may use at most 128 MiB of HBM per device.

```python
import math
import jax
import jax.numpy as jnp
from jax import lax

BLOCK = 112
MEETINGS = 2
NS_STEPS = 2
COLS = 7168
ROWS = 32768


def draw_weight_delta(key, part):
    key = jax.random.fold_in(key, 7)
    keys = jax.random.split(key, 7)
    factor_count = 32
    independent = jnp.clip(jax.random.normal(keys[0], (COLS, ROWS), jnp.float32), -4.0, 4.0)
    row_scale = jnp.exp(jax.random.uniform(keys[1], (1, ROWS), jnp.float32, math.log(0.3), math.log(3.0)))
    loadings = jax.random.uniform(keys[2], (COLS, 1), jnp.float32, 0.6, 1.2)
    col_scale = jnp.exp(jax.random.uniform(keys[3], (COLS, 1), jnp.float32, math.log(0.3), math.log(3.0)))
    groups = jax.random.randint(keys[4], (COLS,), 0, factor_count)
    sign_flip = (jax.random.randint(keys[5], (COLS, 1), 0, 2) * 2 - 1).astype(jnp.float32)
    factors = jnp.clip(jax.random.normal(keys[6], (factor_count, ROWS), jnp.float32), -4.0, 4.0)
    shared = factors[groups]
    values = col_scale * row_scale * (independent + sign_flip * loadings * shared)
    return values.astype(jnp.bfloat16)


def setup_inputs(seed: int = 0) -> dict:
    key_of = jax.random.split(jax.random.key(seed), 2)
    weight_delta = draw_weight_delta(jax.random.fold_in(key_of[1], 71), 0)
    return dict(weight_delta=weight_delta)


eps_value = 1e-06

def rotation(gram):
    pair_width = gram.shape[0]
    identity = jnp.eye(pair_width, dtype=jnp.float32)
    diagonal = jnp.diagonal(gram)
    inverse = lax.rsqrt(diagonal + eps_value)
    norm_root = jnp.sqrt(diagonal + eps_value)
    normed = gram * inverse[:, None] * inverse[None, :]
    row_bound = jnp.max(lax.optimization_barrier(jnp.sum(jnp.abs(normed), axis=1)))
    upper = normed / row_bound
    factor = identity
    for iteration in range(NS_STEPS):
        middle = 1.5 * identity - 0.5 * jnp.dot(factor, upper, precision=lax.Precision.HIGHEST)
        upper = jnp.dot(upper, middle, precision=lax.Precision.HIGHEST)
        factor = jnp.dot(middle, factor, precision=lax.Precision.HIGHEST)
    turning = inverse[:, None] * factor * norm_root[None, :] / jnp.sqrt(row_bound)
    return turning.astype(jnp.bfloat16)

def meeting_update(stacked):
    gram = jnp.dot(stacked, stacked.T, preferred_element_type=jnp.float32)
    turning = rotation(gram)
    updated = lax.dot_general(turning, stacked, (((0,), (0,)), ((), ())), preferred_element_type=jnp.float32)
    updated = updated.astype(jnp.bfloat16)
    return jnp.concatenate([updated[BLOCK:], updated[:BLOCK]], axis=0)

def reference(weight_delta):
    current = weight_delta
    pair_count = COLS // (2 * BLOCK)
    for meeting in range(MEETINGS):
        if meeting % 2 == 0:
            stacked = current.reshape(pair_count, 2 * BLOCK, ROWS)
            current = lax.map(meeting_update, stacked).reshape(COLS, ROWS)
        else:
            interior = current[BLOCK:COLS - BLOCK].reshape(pair_count - 1, 2 * BLOCK, ROWS)
            updated = lax.map(meeting_update, interior).reshape(COLS - 2 * BLOCK, ROWS)
            current = jnp.concatenate([current[:BLOCK], updated, current[COLS - BLOCK:]], axis=0)
    return current
```

```python
import functools

import jax
import jax.numpy as jnp
from jax import lax
from jax.experimental import pallas as pl
from jax.experimental.pallas import tpu as pltpu
from jax.sharding import PartitionSpec as P

BLOCK = 112
PAD = 128
PAIRS = 4
SIDE = 8
CHUNK = 56
GROUPS = 3
EPS = 1e-6
MESH = pl.DeviceIdType.MESH
FAR_FIRST = (4, 3, 5, 2, 6, 1, 7)


def dot(a, b):
    return jnp.dot(a, b, preferred_element_type=jnp.float32)


def dot_nt(a, b):
    return lax.dot_general(a, b, (((1,), (1,)), ((), ())), preferred_element_type=jnp.float32)


def halves(x):
    high = x.astype(jnp.bfloat16)
    low = (x - high.astype(jnp.float32)).astype(jnp.bfloat16)
    return high, low


def dot3(a, b):
    a_high, a_low = a
    b_high, b_low = b
    return dot(a_high, b_high) + (dot(a_high, b_low) + dot(a_low, b_high))


def both_sides(left, x, right):
    high, low = halves(x)
    high, low = halves(dot(left, high) + dot(left, low))
    return dot_nt(high, right) + dot_nt(low, right)


def turning_transposed(gram):
    shape = gram.shape
    eye = lax.broadcasted_iota(jnp.int32, shape, 0) == lax.broadcasted_iota(jnp.int32, shape, 1)
    diagonals = jnp.where(eye, gram, 0.0)
    down = jnp.sum(diagonals, axis=1, keepdims=True) + EPS
    across = jnp.sum(diagonals, axis=0, keepdims=True) + EPS
    inverse_across = lax.rsqrt(across)
    normed = gram * lax.rsqrt(down) * inverse_across
    bound = jnp.max(jnp.sum(jnp.abs(normed), axis=0, keepdims=True), axis=1, keepdims=True)
    upper = normed * (1.0 / bound)
    parts = halves(upper)
    square = dot3(parts, parts)
    rest = dot3(halves(square), halves(-0.5625 * upper + 0.0625 * square))
    factor = jnp.where(eye, 2.25, 0.0) - 2.4375 * upper + 1.6875 * square + rest
    return (factor * (jnp.sqrt(down) * lax.rsqrt(bound)) * inverse_across).astype(jnp.bfloat16)


def tile_iotas():
    return (
        lax.broadcasted_iota(jnp.int32, (PAD, PAD), 0),
        lax.broadcasted_iota(jnp.int32, (PAD, PAD), 1),
    )


def packed(first, last):
    row, column = tile_iotas()
    turned = pltpu.roll(last, PAD - 1, 1)
    return jnp.where((column < row) | (column == PAD - 1), turned, first)[:BLOCK]


def padded(x):
    return jnp.concatenate([x, jnp.zeros((PAD - BLOCK, PAD), jnp.float32)], axis=0)


def unpacked(both):
    row, column = tile_iotas()
    both = padded(both)
    first = jnp.where((column >= row) & (column < BLOCK), both, 0.0)
    first = jnp.where(column >= row, first, first.T)
    last = jnp.where(column <= row, pltpu.roll(both, 1, 1), 0.0)
    last = jnp.where(column <= row, last, last.T)
    return first, last


def square_of(a, b, c, d):
    return jnp.concatenate([jnp.concatenate([a, b], axis=1), jnp.concatenate([c, d], axis=1)], axis=0)


def kernel(
    x_ref, o_ref, own, beside, part, gathered, middle, full, grams, turn, stack, corner, corner_in, turn_in, wide, wide_in,
    staged, in_sem, out_sem, send_sem, recv_sem, side_send, side_recv,
):
    c, r = lax.axis_index("col"), lax.axis_index("row")
    col_count = lax.axis_size("col")
    z, y = lax.div(r, SIDE), lax.rem(r, SIDE)
    left, right = (lax.rem(c + col_count - 1, col_count), r), (lax.rem(c + 1, col_count), r)

    def along_y(step):
        return (c, z * SIDE + lax.rem(y + step, SIDE))

    def along_z(step):
        return (c, lax.rem(z + step, SIDE) * SIDE + y)

    places = ((y, z), (z, y))
    movers = ((along_y, along_z), (along_z, along_y))

    barrier = pltpu.get_barrier_semaphore()
    for step in range(1, SIDE):
        pl.semaphore_signal(barrier, inc=1, device_id=along_y(step), device_id_type=MESH)
        pl.semaphore_signal(barrier, inc=1, device_id=along_z(step), device_id_type=MESH)
    for side in (left, right):
        pl.semaphore_signal(barrier, inc=1, device_id=side, device_id_type=MESH)

    loads = []
    for b in range(2 * PAIRS):
        loads.append(
            pltpu.make_async_copy(
                x_ref.at[pl.ds(b * BLOCK, BLOCK)], own.at[b // 2, pl.ds((b % 2) * PAD, BLOCK)], in_sem.at[b]
            )
        )
        loads[-1].start()
    gap = jnp.zeros((PAD - BLOCK, own.shape[-1]), jnp.bfloat16)
    for lower in (BLOCK, PAD + BLOCK):
        beside[pl.ds(lower, PAD - BLOCK)] = gap
        for k in range(PAIRS):
            own[k, pl.ds(lower, PAD - BLOCK)] = gap

    def sideways(source, target, index, device):
        return pltpu.make_async_remote_copy(
            src_ref=source, dst_ref=target, send_sem=side_send.at[index], recv_sem=side_recv.at[index],
            device_id=device, device_id_type=MESH,
        )

    pair_out = [
        sideways(x_ref.at[pl.ds(b * BLOCK, BLOCK)], beside.at[pl.ds(b * PAD, BLOCK)], b, left) for b in range(2)
    ]
    turn_out = sideways(turn.at[0, pl.ds(PAD, PAD)], turn_in, 2, left)
    corner_out = sideways(corner, corner_in, 3, left)
    block_out = sideways(stack.at[PAIRS, pl.ds(0, PAD)], stack.at[0, pl.ds(0, PAD)], 4, right)
    wide_out = sideways(wide, wide_in, 5, right)

    pl.semaphore_wait(barrier, 2 * (SIDE - 1) + 2)
    for copy in pair_out:
        copy.start()

    def send(group, half, phase, source_of, target):
        mover = movers[half][1 if phase == 1 else 0]
        for step in FAR_FIRST:
            device = mover(step)
            pltpu.make_async_remote_copy(
                src_ref=source_of(step), dst_ref=target,
                send_sem=send_sem.at[group, half, phase], recv_sem=recv_sem.at[group, half, phase],
                device_id=device, device_id_type=MESH,
            ).start()

    def wait(sem, group, half, phase):
        seven = gathered.at[group, half, pl.ds(0, SIDE - 1)]
        pltpu.make_async_copy(seven, seven, sem.at[group, half, phase]).wait()

    def spread(group, half):
        place = places[half][0]
        gathered[group, half, place] = part[group, half * SIDE + place]
        send(
            group, half, 0,
            lambda step: part.at[group, half * SIDE + lax.rem(place + step, SIDE)],
            gathered.at[group, half, place],
        )

    def summed(ref, group, half):
        total = ref[group, half, 0]
        for i in range(1, SIDE):
            total = total + ref[group, half, i]
        return total

    def cross(group, half):
        wait(recv_sem, group, half, 0)
        place = places[half][1]
        middle[group, half, place] = summed(gathered, group, half)
        here = middle.at[group, half, place]
        send(group, half, 1, lambda step: here, here)

    def share(group, half):
        wait(recv_sem, group, half, 1)
        place = half * SIDE + places[half][0]
        full[group, place] = summed(middle, group, half)
        here = full.at[group, place]
        send(group, half, 2, lambda step: here, here)

    def put(group, chunk, x):
        part[group, pl.ds(chunk, 2)] = x[:BLOCK].reshape(2, CHUNK, PAD)

    def take(group, chunk):
        return full[group, pl.ds(chunk, 2)].reshape(BLOCK, PAD)

    for k in range(PAIRS):
        loads[2 * k].wait()
        loads[2 * k + 1].wait()
        pair = own[k]
        gram = dot_nt(pair, pair)
        put(0, 4 * k, packed(gram[:PAD, :PAD], gram[PAD:, PAD:]))
        put(0, 4 * k + 2, gram[:PAD, PAD:])
        if k % 2 == 1:
            spread(0, k // 2)
    for k in range(PAIRS):
        group, half = 1 + k // 2, k % 2
        if k == PAIRS - 1:
            for copy in pair_out:
                copy.wait_recv()
        cross_gram = dot_nt(own[k], own[k + 1] if k < PAIRS - 1 else beside[...])
        put(group, half * SIDE, cross_gram[:PAD, :PAD])
        put(group, half * SIDE + 2, cross_gram[:PAD, PAD:])
        put(group, half * SIDE + 4, cross_gram[PAD:, :PAD])
        put(group, half * SIDE + 6, cross_gram[PAD:, PAD:])
        spread(group, half)
    for group in range(GROUPS):
        for half in range(2):
            cross(group, half)
    for group in range(GROUPS):
        for half in range(2):
            share(group, half)

    for half in range(2):
        wait(recv_sem, 0, half, 2)
    for k in range(PAIRS):
        first, last = unpacked(take(0, 4 * k))
        between = padded(take(0, 4 * k + 2))
        grams[k] = square_of(first, between, between.T, last)
    for k in range(PAIRS):
        turn[k] = turning_transposed(grams[k])
    turn_out.start()
    for k in (PAIRS - 1, 0, 1, 2):
        updated = dot(turn[k], own[k]).astype(jnp.bfloat16)
        stack[k + 1, pl.ds(0, PAD)] = updated[:PAD]
        stack[k, pl.ds(PAD, PAD)] = updated[PAD:]
        if k == PAIRS - 1:
            block_out.start()
    firsts, lasts = [], []
    for k in range(PAIRS):
        firsts.append(both_sides(turn[k, pl.ds(0, PAD)], grams[k], turn[k, pl.ds(0, PAD)]))
        lasts.append(both_sides(turn[k, pl.ds(PAD, PAD)], grams[k], turn[k, pl.ds(PAD, PAD)]))
        if k == 0:
            corner[...] = lasts[0]
            corner_out.start()
    turn_out.wait_recv()
    stack[PAIRS, pl.ds(PAD, PAD)] = dot(turn_in[...], beside[...]).astype(jnp.bfloat16)

    stores = [
        pltpu.make_async_copy(staged.at[b], o_ref.at[pl.ds(b * BLOCK, BLOCK)], out_sem.at[b]) for b in range(2 * PAIRS)
    ]

    def second(k):
        group, half = 1 + k // 2, k % 2
        quarters = [padded(take(group, half * SIDE + 2 * i)) for i in range(4)]
        inner = k < PAIRS - 1
        other = turn[k + 1, pl.ds(PAD, PAD)] if inner else turn_in[...]
        between = both_sides(turn[k, pl.ds(0, PAD)], square_of(*quarters), other)
        last = lasts[k + 1] if inner else corner_in[...]
        return turning_transposed(square_of(firsts[k], between, between.T, last))

    def finish(k, turning):
        updated = dot(turning, stack[k + 1]).astype(jnp.bfloat16)
        staged[2 * k + 1] = updated[PAD : PAD + BLOCK]
        if k < PAIRS - 1:
            staged[2 * k + 2] = updated[:BLOCK]
            stores[2 * k + 2].start()
        else:
            staged[2 * k + 1] = jnp.where(c == col_count - 1, stack[PAIRS, pl.ds(0, BLOCK)], updated[PAD : PAD + BLOCK])
        stores[2 * k + 1].start()

    for half in range(2):
        wait(recv_sem, 1, half, 2)
    for k, turning in enumerate([second(0), second(1)]):
        finish(k, turning)
    for half in range(2):
        wait(recv_sem, 2, half, 2)
    corner_out.wait_recv()
    turning = second(PAIRS - 1)
    wide[...] = turning[:PAD]
    wide_out.start()
    finish(PAIRS - 1, turning)
    finish(2, second(2))
    block_out.wait_recv()
    wide_out.wait_recv()
    first_block = dot(wide_in[...], stack[0]).astype(jnp.bfloat16)[:BLOCK]
    staged[0] = jnp.where(c == 0, stack[0, pl.ds(PAD, BLOCK)], first_block)
    stores[0].start()

    for copy in pair_out + [turn_out, corner_out, block_out, wide_out]:
        copy.wait_send()
    for group in range(GROUPS):
        for half in range(2):
            for phase in range(3):
                wait(send_sem, group, half, phase)
    for copy in stores:
        copy.wait()


def shards(weight_delta):
    width = weight_delta.shape[1]
    chunks = (GROUPS, 2, SIDE, CHUNK, PAD)
    whole = (GROUPS, 2 * SIDE, CHUNK, PAD)
    f32, bf16 = jnp.float32, jnp.bfloat16
    return pl.pallas_call(
        kernel,
        out_shape=jax.ShapeDtypeStruct(weight_delta.shape, bf16),
        in_specs=[pl.BlockSpec(memory_space=pl.ANY)],
        out_specs=pl.BlockSpec(memory_space=pl.ANY),
        scratch_shapes=[
            pltpu.VMEM((PAIRS, 2 * PAD, width), bf16),
            pltpu.VMEM((2 * PAD, width), bf16),
            pltpu.VMEM(whole, f32),
            pltpu.VMEM(chunks, f32),
            pltpu.VMEM(chunks, f32),
            pltpu.VMEM(whole, f32),
            pltpu.VMEM((PAIRS, 2 * PAD, 2 * PAD), f32),
            pltpu.VMEM((PAIRS, 2 * PAD, 2 * PAD), bf16),
            pltpu.VMEM((PAIRS + 1, 2 * PAD, width), bf16),
            pltpu.VMEM((PAD, PAD), f32),
            pltpu.VMEM((PAD, PAD), f32),
            pltpu.VMEM((PAD, 2 * PAD), bf16),
            pltpu.VMEM((PAD, 2 * PAD), bf16),
            pltpu.VMEM((PAD, 2 * PAD), bf16),
            pltpu.VMEM((2 * PAIRS, BLOCK, width), bf16),
            pltpu.SemaphoreType.DMA((2 * PAIRS,)),
            pltpu.SemaphoreType.DMA((2 * PAIRS,)),
            pltpu.SemaphoreType.DMA((GROUPS, 2, 3)),
            pltpu.SemaphoreType.DMA((GROUPS, 2, 3)),
            pltpu.SemaphoreType.DMA((6,)),
            pltpu.SemaphoreType.DMA((6,)),
        ],
        compiler_params=pltpu.CompilerParams(
            collective_id=0, has_side_effects=True, vmem_limit_bytes=40 * 2**20
        ),
    )(weight_delta)


def solution(mesh):
    return jax.shard_map(
        shards, mesh=mesh, in_specs=(P("col", "row"),), out_specs=P("col", "row"), check_vma=False
    )
```

```python
import functools

import jax
import jax.numpy as jnp
from jax import lax
from jax.experimental import pallas as pl
from jax.experimental.pallas import tpu as pltpu
from jax.sharding import PartitionSpec as P

BLOCK = 112
PAD = 128
PAIRS = 4
SIDE = 8
CHUNK = 56
TILE = 8
GROUPS = 3
EPS = 1e-6
STAGE, LAG, TURN = 10, 5, 60.5
CROSS_ORDER = (0, 3, 1, 2)
CROSS_PLACE = {0: (1, 0), 3: (1, 1), 1: (2, 0), 2: (2, 1)}
MESH = pl.DeviceIdType.MESH
FAR_FIRST = (4, 3, 5, 2, 6, 1, 7)


def dot(a, b):
    return jnp.dot(a, b, preferred_element_type=jnp.float32)


def dot_nt(a, b):
    return lax.dot_general(a, b, (((1,), (1,)), ((), ())), preferred_element_type=jnp.float32)


def halves(x):
    high = x.astype(jnp.bfloat16)
    low = (x - high.astype(jnp.float32)).astype(jnp.bfloat16)
    return high, low


def dot3(a, b):
    a_high, a_low = a
    b_high, b_low = b
    return dot(
        jnp.concatenate([a_high, a_high, a_low], axis=1), jnp.concatenate([b_high, b_low, b_high], axis=0)
    )


def both_sides(left, x, right):
    product = dot(jnp.concatenate([left, left], axis=1), jnp.concatenate(halves(x), axis=0))
    return dot_nt(jnp.concatenate(halves(product), axis=1), jnp.concatenate([right, right], axis=1))


def turning_transposed(gram):
    shape = gram.shape
    eye = lax.broadcasted_iota(jnp.int32, shape, 0) == lax.broadcasted_iota(jnp.int32, shape, 1)
    small_eye = eye[:PAD, :PAD]
    corners = [jnp.where(small_eye, gram[i : i + PAD, i : i + PAD], 0.0) for i in (0, PAD)]
    down = jnp.concatenate([jnp.sum(x, axis=1, keepdims=True) for x in corners], axis=0) + EPS
    across = jnp.concatenate([jnp.sum(x, axis=0, keepdims=True) for x in corners], axis=1) + EPS
    inverse_across = lax.rsqrt(across)
    normed = gram * lax.rsqrt(down) * inverse_across
    parts = halves(normed)
    square = dot3(parts, parts)
    bound = jnp.max(jnp.sum(jnp.abs(normed), axis=0, keepdims=True), axis=1, keepdims=True)
    share = 1.0 / bound
    share2 = share * share
    rest = dot3(halves(square), halves((-0.5625 * share * share2) * normed + (0.0625 * share2 * share2) * square))
    factor = jnp.where(eye, 2.25, 0.0) + (-2.4375 * share) * normed + (1.6875 * share2) * square + rest
    return (factor * (jnp.sqrt(down) * lax.rsqrt(bound)) * inverse_across).astype(jnp.bfloat16)


def tile_iotas():
    return (
        lax.broadcasted_iota(jnp.int32, (PAD, PAD), 0),
        lax.broadcasted_iota(jnp.int32, (PAD, PAD), 1),
    )


def packed(first, last):
    row, column = tile_iotas()
    turned = pltpu.roll(last, PAD - 1, 1)
    return jnp.where((column < row) | (column == PAD - 1), turned, first)[:BLOCK]


def padded(x):
    return jnp.concatenate([x, jnp.zeros((PAD - BLOCK, PAD), jnp.float32)], axis=0)


def unpacked(both):
    row, column = tile_iotas()
    both = padded(both)
    first = jnp.where((column >= row) & (column < BLOCK), both, 0.0)
    first = jnp.where(column >= row, first, first.T)
    last = jnp.where(column <= row, pltpu.roll(both, 1, 1), 0.0)
    last = jnp.where(column <= row, last, last.T)
    return first, last


def square_of(a, b, c, d):
    return jnp.concatenate([jnp.concatenate([a, b], axis=1), jnp.concatenate([c, d], axis=1)], axis=0)


def kernel(
    x_ref, o_ref, own, beside, part, relay_in, relay_out, final_in, middle, tiles, full, grams, turn, stack, corner,
    corner_in, turn_in, wide, wide_in, in_sem, send_sem, recv_sem, side_send, side_recv,
):
    c, r = lax.axis_index("col"), lax.axis_index("row")
    col_count = lax.axis_size("col")
    z, y = lax.div(r, SIDE), lax.rem(r, SIDE)
    left, right = (lax.rem(c + col_count - 1, col_count), r), (lax.rem(c + 1, col_count), r)
    tie = 2 * lax.rem(c, 2) - 1

    def ring(place, step):
        return lax.rem(place + step + SIDE, SIDE)

    def along_y(step):
        return (c, z * SIDE + ring(y, step))

    def along_z(step):
        return (c, ring(z, step) * SIDE + y)

    places = ((y, z), (z, y))
    movers = ((along_y, along_z), (along_z, along_y))

    barrier = pltpu.get_barrier_semaphore()
    for step in range(1, SIDE):
        pl.semaphore_signal(barrier, inc=1, device_id=along_y(step), device_id_type=MESH)
        pl.semaphore_signal(barrier, inc=1, device_id=along_z(step), device_id_type=MESH)
    for side in (left, right):
        pl.semaphore_signal(barrier, inc=1, device_id=side, device_id_type=MESH)

    loads = []
    for b in range(2 * PAIRS):
        loads.append(
            pltpu.make_async_copy(
                x_ref.at[pl.ds(b * BLOCK, BLOCK)], own.at[b // 2, pl.ds((b % 2) * PAD, BLOCK)], in_sem.at[b]
            )
        )
        loads[-1].start()
    gap = jnp.zeros((PAD - BLOCK, own.shape[-1]), jnp.bfloat16)
    for lower in (BLOCK, PAD + BLOCK):
        beside[pl.ds(lower, PAD - BLOCK)] = gap
        for k in range(PAIRS):
            own[k, pl.ds(lower, PAD - BLOCK)] = gap
    for group in range(GROUPS):
        for half in range(2):
            middle[group, half, SIDE - 1] = jnp.zeros((TILE, PAD), jnp.float32)

    def sideways(source, target, index, device):
        return pltpu.make_async_remote_copy(
            src_ref=source, dst_ref=target, send_sem=side_send.at[index], recv_sem=side_recv.at[index],
            device_id=device, device_id_type=MESH,
        )

    pair_out = [
        sideways(x_ref.at[pl.ds(b * BLOCK, BLOCK)], beside.at[pl.ds(b * PAD, BLOCK)], b, left) for b in range(2)
    ]
    turn_out = sideways(turn.at[0, pl.ds(PAD, PAD)], turn_in, 2, left)
    corner_out = sideways(corner, corner_in, 3, left)
    block_out = sideways(stack.at[PAIRS, pl.ds(0, PAD)], stack.at[0, pl.ds(0, PAD)], 4, right)
    wide_out = sideways(wide, wide_in, 5, right)

    pl.semaphore_wait(barrier, 2 * (SIDE - 1) + 2)
    for copy in pair_out:
        copy.start()

    def send(group, half, axis, step, source, target, kind, small=0):
        pltpu.make_async_remote_copy(
            src_ref=source, dst_ref=target, send_sem=send_sem.at[group, half, small],
            recv_sem=recv_sem.at[group, half, kind], device_id=movers[half][axis](step), device_id_type=MESH,
        ).start()

    def arrived(like, group, half, kind):
        pltpu.make_async_copy(like, like, recv_sem.at[group, half, kind]).wait()

    def chunk_of(ref, group, half, step):
        return ref.at[group, half * SIDE + ring(places[half][0], step), pl.ds(0, CHUNK)]

    def spread(group, half):
        send(group, half, 0, 2 * tie, chunk_of(part, group, half, 4), relay_in.at[group, half, 2], 0)
        for slot, step in enumerate((1, -1)):
            send(group, half, 0, step, chunk_of(part, group, half, 3 * step), relay_in.at[group, half, slot], 0)
        for slot, step in enumerate((1, -1)):
            send(group, half, 0, step, chunk_of(part, group, half, step), final_in.at[group, half, slot], 1)

    def relay(group, half):
        arrived(relay_in.at[group, half], group, half, 0)
        for slot, step in enumerate((1, -1)):
            here = chunk_of(part, group, half, 2 * step)[...] + relay_in[group, half, slot]
            relay_out[group, half, slot] = here + jnp.where(tie == step, relay_in[group, half, 2], 0.0)
            send(group, half, 0, 2 * step, relay_out.at[group, half, slot], final_in.at[group, half, 2 + slot], 1)

    def cross(group, half):
        arrived(final_in.at[group, half], group, half, 1)
        total = chunk_of(part, group, half, 0)[...]
        for slot in range(4):
            total = total + final_in[group, half, slot]
        middle[group, half, pl.ds(0, SIDE - 1)] = total.reshape(SIDE - 1, TILE, PAD)
        place = places[half][1]
        for step in FAR_FIRST:
            send(
                group, half, 1, step, middle.at[group, half, ring(place, step)], tiles.at[group, half, place], 2, 1
            )
        tiles[group, half, place] = middle[group, half, place]

    def back(group, half):
        arrived(tiles.at[group, half, pl.ds(0, SIDE - 1)], group, half, 2)
        total = tiles[group, half, 0]
        for i in range(1, SIDE):
            total = total + tiles[group, half, i]
        first, second = places[half]
        here = full.at[group, half * SIDE + first, pl.ds(pl.multiple_of(second * TILE, TILE), TILE)]
        here[...] = total
        for step in FAR_FIRST:
            send(group, half, 1, step, here, here, 3, 1)

    def share(group, half):
        arrived(tiles.at[group, half, pl.ds(0, SIDE - 1)], group, half, 3)
        here = chunk_of(full, group, half, 0)
        for step in (2, -2):
            send(group, half, 0, step, here, here, 4)
        for step in (1, -1):
            send(group, half, 0, step, here, here, 5)

    def pass_on(group, half):
        arrived(final_in.at[group, half, pl.ds(0, 2)], group, half, 4)
        here = chunk_of(full, group, half, -2 * tie)
        send(group, half, 0, 2 * tie, here, here, 5)
        for step in (1, -1):
            here = chunk_of(full, group, half, -2 * step)
            send(group, half, 0, step, here, here, 5)

    def complete(group, half):
        arrived(full.at[group, pl.ds(0, 5), pl.ds(0, CHUNK)], group, half, 5)

    def put(group, chunk, x):
        part[group, pl.ds(chunk, 2)] = x[:BLOCK].reshape(2, CHUNK, PAD)

    def take(group, chunk):
        return full[group, pl.ds(chunk, 2), pl.ds(0, CHUNK)].reshape(BLOCK, PAD)

    firsts, lasts, turnings = {}, {}, {}

    def gram_products(half):
        for k in (2 * half, 2 * half + 1):
            loads[2 * k].wait()
            loads[2 * k + 1].wait()
            pair = own[k]
            gram = dot_nt(pair, pair)
            put(0, 4 * k, packed(gram[:PAD, :PAD], gram[PAD:, PAD:]))
            put(0, 4 * k + 2, gram[:PAD, PAD:])
        spread(0, half)

    def cross_products(k):
        group, half = CROSS_PLACE[k]
        if k == PAIRS - 1:
            for copy in pair_out:
                copy.wait_recv()
        gram = dot_nt(own[k], own[k + 1] if k < PAIRS - 1 else beside[...])
        put(group, half * SIDE, gram[:PAD, :PAD])
        put(group, half * SIDE + 2, gram[:PAD, PAD:])
        put(group, half * SIDE + 4, gram[PAD:, :PAD])
        put(group, half * SIDE + 6, gram[PAD:, PAD:])
        spread(group, half)

    def first_turnings():
        for k in range(PAIRS):
            first, last = unpacked(take(0, 4 * k))
            between = padded(take(0, 4 * k + 2))
            grams[k] = square_of(first, between, between.T, last)
        for k in range(PAIRS):
            turn[k] = turning_transposed(grams[k])
        turn_out.start()

    def first_update(k):
        updated = dot(turn[k], own[k]).astype(jnp.bfloat16)
        stack[k + 1, pl.ds(0, PAD)] = updated[:PAD]
        stack[k, pl.ds(PAD, PAD)] = updated[PAD:]

    def turned_grams():
        for k in range(PAIRS):
            firsts[k] = both_sides(turn[k, pl.ds(0, PAD)], grams[k], turn[k, pl.ds(0, PAD)])
            lasts[k] = both_sides(turn[k, pl.ds(PAD, PAD)], grams[k], turn[k, pl.ds(PAD, PAD)])
        corner[...] = lasts[0]
        first_update(PAIRS - 1)
        corner_out.start()
        block_out.start()

    def first_updates():
        for k in range(PAIRS - 1):
            first_update(k)

    def update_beside():
        stack[PAIRS, pl.ds(PAD, PAD)] = dot(turn_in[...], beside[...]).astype(jnp.bfloat16)

    def second_turnings(*pairs):
        if PAIRS - 1 in pairs:
            turn_out.wait_recv()
            corner_out.wait_recv()
        between = {}
        for k in pairs:
            group, half = CROSS_PLACE[k]
            cross_gram = square_of(*[padded(take(group, half * SIDE + 2 * i)) for i in range(4)])
            other = turn[k + 1, pl.ds(PAD, PAD)] if k < PAIRS - 1 else turn_in[...]
            between[k] = both_sides(turn[k, pl.ds(0, PAD)], cross_gram, other)
        for k in pairs:
            last = lasts[k + 1] if k < PAIRS - 1 else corner_in[...]
            turnings[k] = turning_transposed(square_of(firsts[k], between[k], between[k].T, last))
        if PAIRS - 1 in pairs:
            wide[...] = turnings[PAIRS - 1][:PAD]
            wide_out.start()
    def second_update(k):
        updated = dot(turnings[k], stack[k + 1]).astype(jnp.bfloat16)
        if k < PAIRS - 1:
            o_ref[pl.ds((2 * k + 1) * BLOCK, BLOCK)] = updated[PAD : PAD + BLOCK]
            o_ref[pl.ds((2 * k + 2) * BLOCK, BLOCK)] = updated[:BLOCK]
        else:
            o_ref[pl.ds((2 * k + 1) * BLOCK, BLOCK)] = jnp.where(c == col_count - 1, stack[PAIRS, pl.ds(0, BLOCK)], updated[PAD : PAD + BLOCK])

    def first_block():
        block_out.wait_recv()
        wide_out.wait_recv()
        updated = dot(wide_in[...], stack[0]).astype(jnp.bfloat16)[:BLOCK]
        o_ref[pl.ds(0, BLOCK)] = jnp.where(c == 0, stack[0, pl.ds(PAD, BLOCK)], updated)

    plan = [(0, gram_products, 0), (0, gram_products, 1)]
    plan += [(LAG, cross_products, k) for k in CROSS_ORDER]
    units = [(0, 0), (0, 1)] + [CROSS_PLACE[k] for k in CROSS_ORDER]
    for i, unit in enumerate(units):
        for j, stage in enumerate((relay, cross, back, share, pass_on, complete)):
            plan.append(((j + 1) * STAGE + (LAG if i >= 2 else 0), stage, *unit))
    plan.append((TURN, first_turnings))
    plan.append((TURN, turned_grams))
    plan.append((100, second_turnings, *CROSS_ORDER))
    plan.append((100, first_updates))
    plan.append((100, update_beside))
    plan += [(100, second_update, k) for k in range(PAIRS)]
    plan.append((100, first_block))
    for _, step, *where in sorted(plan, key=lambda entry: entry[0]):
        step(*where)

    for copy in pair_out + [turn_out, corner_out, block_out, wide_out]:
        copy.wait_send()
    for group in range(GROUPS):
        for half in range(2):
            for small, like in enumerate((full.at[group, pl.ds(0, 14), pl.ds(0, CHUNK)], part.at[group, pl.ds(0, 2)])):
                pltpu.make_async_copy(like, like, send_sem.at[group, half, small]).wait()


def shards(weight_delta):
    width = weight_delta.shape[1]
    chunks = lambda count: pltpu.VMEM((GROUPS, 2, count, CHUNK, PAD), f32)
    f32, bf16 = jnp.float32, jnp.bfloat16
    return pl.pallas_call(
        kernel,
        out_shape=pltpu.VMEM(weight_delta.shape, bf16),
        in_specs=[pl.BlockSpec(memory_space=pl.ANY)],
        out_specs=pl.BlockSpec(memory_space=pltpu.VMEM),
        scratch_shapes=[
            pltpu.VMEM((PAIRS, 2 * PAD, width), bf16),
            pltpu.VMEM((2 * PAD, width), bf16),
            pltpu.VMEM((GROUPS, 2 * SIDE, CHUNK, PAD), f32),
            chunks(3),
            chunks(2),
            chunks(4),
            pltpu.VMEM((GROUPS, 2, SIDE, TILE, PAD), f32),
            pltpu.VMEM((GROUPS, 2, SIDE, TILE, PAD), f32),
            pltpu.VMEM((GROUPS, 2 * SIDE, SIDE * TILE, PAD), f32),
            pltpu.VMEM((PAIRS, 2 * PAD, 2 * PAD), f32),
            pltpu.VMEM((PAIRS, 2 * PAD, 2 * PAD), bf16),
            pltpu.VMEM((PAIRS + 1, 2 * PAD, width), bf16),
            pltpu.VMEM((PAD, PAD), f32),
            pltpu.VMEM((PAD, PAD), f32),
            pltpu.VMEM((PAD, 2 * PAD), bf16),
            pltpu.VMEM((PAD, 2 * PAD), bf16),
            pltpu.VMEM((PAD, 2 * PAD), bf16),
            pltpu.SemaphoreType.DMA((2 * PAIRS,)),
            pltpu.SemaphoreType.DMA((GROUPS, 2, 2)),
            pltpu.SemaphoreType.DMA((GROUPS, 2, 6)),
            pltpu.SemaphoreType.DMA((6,)),
            pltpu.SemaphoreType.DMA((6,)),
        ],
        compiler_params=pltpu.CompilerParams(
            collective_id=0, has_side_effects=True, vmem_limit_bytes=58 * 2**20
        ),
    )(weight_delta)


def solution(mesh):
    return jax.shard_map(
        shards, mesh=mesh, in_specs=(P("col", "row"),), out_specs=P("col", "row"), check_vma=False
    )
```

```python
import functools

import jax
import jax.numpy as jnp
from jax import lax
from jax.experimental import pallas as pl
from jax.experimental.pallas import tpu as pltpu
from jax.sharding import PartitionSpec as P

BLOCK = 112
PAD = 128
PAIRS = 4
SIDE = 8
CHUNK = 56
TILE = 8
GROUPS = 3
EPS = 1e-6
STAGE, LAG, TURN = 10, 5, 60.5
CROSS_ORDER = (0, 1, 3, 2)
CROSS_PLACE = {0: (1, 0), 1: (1, 1), 3: (2, 0), 2: (2, 1)}
MESH = pl.DeviceIdType.MESH
FAR_FIRST = (4, 3, 5, 2, 6, 1, 7)


def dot(a, b):
    return jnp.dot(a, b, preferred_element_type=jnp.float32)


def dot_nt(a, b):
    return lax.dot_general(a, b, (((1,), (1,)), ((), ())), preferred_element_type=jnp.float32)


def halves(x):
    high = x.astype(jnp.bfloat16)
    low = (x - high.astype(jnp.float32)).astype(jnp.bfloat16)
    return high, low


def dot3(a, b):
    a_high, a_low = a
    b_high, b_low = b
    return dot(
        jnp.concatenate([a_high, a_high, a_low], axis=1), jnp.concatenate([b_high, b_low, b_high], axis=0)
    )


def both_sides(left, x, right):
    product = dot(jnp.concatenate([left, left], axis=1), jnp.concatenate(halves(x), axis=0))
    return dot_nt(jnp.concatenate(halves(product), axis=1), jnp.concatenate([right, right], axis=1))


def turning_transposed(gram):
    shape = gram.shape
    eye = lax.broadcasted_iota(jnp.int32, shape, 0) == lax.broadcasted_iota(jnp.int32, shape, 1)
    small_eye = eye[:PAD, :PAD]
    corners = [jnp.where(small_eye, gram[i : i + PAD, i : i + PAD], 0.0) for i in (0, PAD)]
    down = jnp.concatenate([jnp.sum(x, axis=1, keepdims=True) for x in corners], axis=0) + EPS
    across = jnp.concatenate([jnp.sum(x, axis=0, keepdims=True) for x in corners], axis=1) + EPS
    inverse_across = lax.rsqrt(across)
    normed = gram * lax.rsqrt(down) * inverse_across
    parts = halves(normed)
    square = dot3(parts, parts)
    bound = jnp.max(jnp.sum(jnp.abs(normed), axis=0, keepdims=True), axis=1, keepdims=True)
    share = 1.0 / bound
    share2 = share * share
    rest = dot3(halves(square), halves((-0.5625 * share * share2) * normed + (0.0625 * share2 * share2) * square))
    factor = jnp.where(eye, 2.25, 0.0) + (-2.4375 * share) * normed + (1.6875 * share2) * square + rest
    return (factor * (jnp.sqrt(down) * lax.rsqrt(bound)) * inverse_across).astype(jnp.bfloat16)


def tile_iotas():
    return (
        lax.broadcasted_iota(jnp.int32, (PAD, PAD), 0),
        lax.broadcasted_iota(jnp.int32, (PAD, PAD), 1),
    )


def packed(first, last):
    row, column = tile_iotas()
    turned = pltpu.roll(last, PAD - 1, 1)
    return jnp.where((column < row) | (column == PAD - 1), turned, first)[:BLOCK]


def padded(x):
    return jnp.concatenate([x, jnp.zeros((PAD - BLOCK, PAD), jnp.float32)], axis=0)


def unpacked(both):
    row, column = tile_iotas()
    both = padded(both)
    first = jnp.where((column >= row) & (column < BLOCK), both, 0.0)
    first = jnp.where(column >= row, first, first.T)
    last = jnp.where(column <= row, pltpu.roll(both, 1, 1), 0.0)
    last = jnp.where(column <= row, last, last.T)
    return first, last


def square_of(a, b, c, d):
    return jnp.concatenate([jnp.concatenate([a, b], axis=1), jnp.concatenate([c, d], axis=1)], axis=0)


def kernel(
    x_ref, o_ref, own, beside, part, relay_in, relay_out, final_in, middle, tiles, full, grams, turn, stack, corner,
    corner_in, turn_in, wide, wide_in, in_sem, send_sem, recv_sem, side_send, side_recv,
):
    c, r = lax.axis_index("col"), lax.axis_index("row")
    col_count = lax.axis_size("col")
    z, y = lax.div(r, SIDE), lax.rem(r, SIDE)
    left, right = (lax.rem(c + col_count - 1, col_count), r), (lax.rem(c + 1, col_count), r)
    tie = 2 * lax.rem(c, 2) - 1

    def ring(place, step):
        return lax.rem(place + step + SIDE, SIDE)

    def along_y(step):
        return (c, z * SIDE + ring(y, step))

    def along_z(step):
        return (c, ring(z, step) * SIDE + y)

    places = ((y, z), (z, y))
    movers = ((along_y, along_z), (along_z, along_y))

    barrier = pltpu.get_barrier_semaphore()
    for step in range(1, SIDE):
        pl.semaphore_signal(barrier, inc=1, device_id=along_y(step), device_id_type=MESH)
        pl.semaphore_signal(barrier, inc=1, device_id=along_z(step), device_id_type=MESH)
    for side in (left, right):
        pl.semaphore_signal(barrier, inc=1, device_id=side, device_id_type=MESH)

    loads = []
    for b in range(2 * PAIRS):
        loads.append(
            pltpu.make_async_copy(
                x_ref.at[pl.ds(b * BLOCK, BLOCK)], own.at[b // 2, pl.ds((b % 2) * PAD, BLOCK)], in_sem.at[b]
            )
        )
        loads[-1].start()
    gap = jnp.zeros((PAD - BLOCK, own.shape[-1]), jnp.bfloat16)
    for lower in (BLOCK, PAD + BLOCK):
        beside[pl.ds(lower, PAD - BLOCK)] = gap
        for k in range(PAIRS):
            own[k, pl.ds(lower, PAD - BLOCK)] = gap
    for group in range(GROUPS):
        for half in range(2):
            middle[group, half, SIDE - 1] = jnp.zeros((TILE, PAD), jnp.float32)

    def sideways(source, target, index, device):
        return pltpu.make_async_remote_copy(
            src_ref=source, dst_ref=target, send_sem=side_send.at[index], recv_sem=side_recv.at[index],
            device_id=device, device_id_type=MESH,
        )

    pair_out = [
        sideways(x_ref.at[pl.ds(b * BLOCK, BLOCK)], beside.at[pl.ds(b * PAD, BLOCK)], b, left) for b in range(2)
    ]
    turn_out = sideways(turn.at[0, pl.ds(PAD, PAD)], turn_in, 2, left)
    corner_out = sideways(corner, corner_in, 3, left)
    block_out = sideways(stack.at[PAIRS, pl.ds(0, PAD)], stack.at[0, pl.ds(0, PAD)], 4, right)
    wide_out = sideways(wide, wide_in, 5, right)

    def send(group, half, axis, step, source, target, kind, small=0):
        pltpu.make_async_remote_copy(
            src_ref=source, dst_ref=target, send_sem=send_sem.at[group, half, small],
            recv_sem=recv_sem.at[group, half, kind], device_id=movers[half][axis](step), device_id_type=MESH,
        ).start()

    def arrived(like, group, half, kind):
        pltpu.make_async_copy(like, like, recv_sem.at[group, half, kind]).wait()

    def chunk_of(ref, group, half, step):
        return ref.at[group, half * SIDE + ring(places[half][0], step), pl.ds(0, CHUNK)]

    def spread(group, half):
        send(group, half, 0, 2 * tie, chunk_of(part, group, half, 4), relay_in.at[group, half, 2], 0)
        for slot, step in enumerate((1, -1)):
            send(group, half, 0, step, chunk_of(part, group, half, 3 * step), relay_in.at[group, half, slot], 0)
        for slot, step in enumerate((1, -1)):
            send(group, half, 0, step, chunk_of(part, group, half, step), final_in.at[group, half, slot], 1)

    def relay(group, half):
        arrived(relay_in.at[group, half], group, half, 0)
        for slot, step in enumerate((1, -1)):
            here = chunk_of(part, group, half, 2 * step)[...] + relay_in[group, half, slot]
            relay_out[group, half, slot] = here + jnp.where(tie == step, relay_in[group, half, 2], 0.0)
            send(group, half, 0, 2 * step, relay_out.at[group, half, slot], final_in.at[group, half, 2 + slot], 1)

    def cross(group, half):
        arrived(final_in.at[group, half], group, half, 1)
        total = chunk_of(part, group, half, 0)[...]
        for slot in range(4):
            total = total + final_in[group, half, slot]
        middle[group, half, pl.ds(0, SIDE - 1)] = total.reshape(SIDE - 1, TILE, PAD)
        place = places[half][1]
        for step in FAR_FIRST:
            send(
                group, half, 1, step, middle.at[group, half, ring(place, step)], tiles.at[group, half, place], 2, 1
            )
        tiles[group, half, place] = middle[group, half, place]

    def back(group, half):
        arrived(tiles.at[group, half, pl.ds(0, SIDE - 1)], group, half, 2)
        total = tiles[group, half, 0]
        for i in range(1, SIDE):
            total = total + tiles[group, half, i]
        first, second = places[half]
        here = full.at[group, half * SIDE + first, pl.ds(pl.multiple_of(second * TILE, TILE), TILE)]
        here[...] = total
        for step in FAR_FIRST:
            send(group, half, 1, step, here, here, 3, 1)

    def share(group, half):
        arrived(tiles.at[group, half, pl.ds(0, SIDE - 1)], group, half, 3)
        here = chunk_of(full, group, half, 0)
        for step in (2, -2):
            send(group, half, 0, step, here, here, 4)
        for step in (1, -1):
            send(group, half, 0, step, here, here, 5)

    def pass_on(group, half):
        arrived(final_in.at[group, half, pl.ds(0, 2)], group, half, 4)
        here = chunk_of(full, group, half, -2 * tie)
        send(group, half, 0, 2 * tie, here, here, 5)
        for step in (1, -1):
            here = chunk_of(full, group, half, -2 * step)
            send(group, half, 0, step, here, here, 5)

    def complete(group, half):
        arrived(full.at[group, pl.ds(0, 5), pl.ds(0, CHUNK)], group, half, 5)

    def put(group, chunk, x):
        part[group, pl.ds(chunk, 2)] = x[:BLOCK].reshape(2, CHUNK, PAD)

    def take(group, chunk):
        return full[group, pl.ds(chunk, 2), pl.ds(0, CHUNK)].reshape(BLOCK, PAD)

    firsts, lasts, turnings = {}, {}, {}

    def gram_products():
        for k in range(PAIRS):
            loads[2 * k].wait()
            loads[2 * k + 1].wait()
            pair = own[k]
            gram = dot_nt(pair, pair)
            put(0, 4 * k, packed(gram[:PAD, :PAD], gram[PAD:, PAD:]))
            put(0, 4 * k + 2, gram[:PAD, PAD:])

    def begin():
        pl.semaphore_wait(barrier, 2 * (SIDE - 1) + 2)
        for copy in pair_out:
            copy.start()
        for half in range(2):
            spread(0, half)

    def cross_products(k):
        group, half = CROSS_PLACE[k]
        if k == PAIRS - 1:
            for copy in pair_out:
                copy.wait_recv()
        gram = dot_nt(own[k], own[k + 1] if k < PAIRS - 1 else beside[...])
        put(group, half * SIDE, gram[:PAD, :PAD])
        put(group, half * SIDE + 2, gram[:PAD, PAD:])
        put(group, half * SIDE + 4, gram[PAD:, :PAD])
        put(group, half * SIDE + 6, gram[PAD:, PAD:])
        spread(group, half)

    def first_turnings(*pairs):
        for k in pairs:
            first, last = unpacked(take(0, 4 * k))
            between = padded(take(0, 4 * k + 2))
            grams[k] = square_of(first, between, between.T, last)
        for k in pairs:
            turn[k] = turning_transposed(grams[k])
        if 0 in pairs:
            turn_out.start()

    def first_update(k):
        updated = dot(turn[k], own[k]).astype(jnp.bfloat16)
        stack[k + 1, pl.ds(0, PAD)] = updated[:PAD]
        stack[k, pl.ds(PAD, PAD)] = updated[PAD:]

    def turned_grams(*pairs):
        for k in pairs:
            lasts[k] = both_sides(turn[k, pl.ds(PAD, PAD)], grams[k], turn[k, pl.ds(PAD, PAD)])
        if 0 in pairs:
            corner[...] = lasts[0]
            corner_out.start()
        for k in pairs:
            firsts[k] = both_sides(turn[k, pl.ds(0, PAD)], grams[k], turn[k, pl.ds(0, PAD)])
        if PAIRS - 1 in pairs:
            first_update(PAIRS - 1)
            block_out.start()

    def first_updates():
        for k in range(PAIRS - 1):
            first_update(k)

    def update_beside():
        stack[PAIRS, pl.ds(PAD, PAD)] = dot(turn_in[...], beside[...]).astype(jnp.bfloat16)

    def second_turnings(*pairs):
        if PAIRS - 1 in pairs:
            turn_out.wait_recv()
            corner_out.wait_recv()
        between = {}
        for k in pairs:
            group, half = CROSS_PLACE[k]
            cross_gram = square_of(*[padded(take(group, half * SIDE + 2 * i)) for i in range(4)])
            other = turn[k + 1, pl.ds(PAD, PAD)] if k < PAIRS - 1 else turn_in[...]
            between[k] = both_sides(turn[k, pl.ds(0, PAD)], cross_gram, other)
        for k in pairs:
            last = lasts[k + 1] if k < PAIRS - 1 else corner_in[...]
            turnings[k] = turning_transposed(square_of(firsts[k], between[k], between[k].T, last))
        if PAIRS - 1 in pairs:
            wide[...] = turnings[PAIRS - 1][:PAD]
            wide_out.start()
    def second_update(k):
        updated = dot(turnings[k], stack[k + 1]).astype(jnp.bfloat16)
        if k < PAIRS - 1:
            o_ref[pl.ds((2 * k + 1) * BLOCK, BLOCK)] = updated[PAD : PAD + BLOCK]
            o_ref[pl.ds((2 * k + 2) * BLOCK, BLOCK)] = updated[:BLOCK]
        else:
            o_ref[pl.ds((2 * k + 1) * BLOCK, BLOCK)] = jnp.where(c == col_count - 1, stack[PAIRS, pl.ds(0, BLOCK)], updated[PAD : PAD + BLOCK])

    def first_block():
        block_out.wait_recv()
        wide_out.wait_recv()
        updated = dot(wide_in[...], stack[0]).astype(jnp.bfloat16)[:BLOCK]
        o_ref[pl.ds(0, BLOCK)] = jnp.where(c == 0, stack[0, pl.ds(PAD, BLOCK)], updated)

    plan = [(0, gram_products), (0, begin)]
    plan += [(LAG, cross_products, k) for k in CROSS_ORDER]
    units = [(0, 0), (0, 1)] + [CROSS_PLACE[k] for k in CROSS_ORDER]
    for i, unit in enumerate(units):
        for j, stage in enumerate((relay, cross, back, share, pass_on, complete)):
            plan.append(((j + 1) * STAGE + (LAG if i >= 2 else 0), stage, *unit))
    plan.append((54.9, complete, 0, 0))
    plan.append((54.9, first_turnings, 0))
    plan.append((54.9, turned_grams, 0))
    plan.append((TURN, first_turnings, 1, 2, 3))
    plan.append((TURN, turned_grams, 1, 2, 3))
    plan.append((100, second_turnings, 3))
    plan.append((100, second_turnings, 0, 1, 2))
    plan.append((100, first_updates))
    plan.append((100, update_beside))
    plan += [(100, second_update, k) for k in range(PAIRS)]
    plan.append((100, first_block))
    plan.remove((6 * STAGE, complete, 0, 0))
    for _, step, *where in sorted(plan, key=lambda entry: entry[0]):
        step(*where)

    for copy in pair_out + [turn_out, corner_out, block_out, wide_out]:
        copy.wait_send()
    for group in range(GROUPS):
        for half in range(2):
            for small, like in enumerate((full.at[group, pl.ds(0, 14), pl.ds(0, CHUNK)], part.at[group, pl.ds(0, 2)])):
                pltpu.make_async_copy(like, like, send_sem.at[group, half, small]).wait()


def shards(weight_delta):
    width = weight_delta.shape[1]
    chunks = lambda count: pltpu.VMEM((GROUPS, 2, count, CHUNK, PAD), f32)
    f32, bf16 = jnp.float32, jnp.bfloat16
    return pl.pallas_call(
        kernel,
        out_shape=pltpu.VMEM(weight_delta.shape, bf16),
        in_specs=[pl.BlockSpec(memory_space=pl.ANY)],
        out_specs=pl.BlockSpec(memory_space=pltpu.VMEM),
        scratch_shapes=[
            pltpu.VMEM((PAIRS, 2 * PAD, width), bf16),
            pltpu.VMEM((2 * PAD, width), bf16),
            pltpu.VMEM((GROUPS, 2 * SIDE, CHUNK, PAD), f32),
            chunks(3),
            chunks(2),
            chunks(4),
            pltpu.VMEM((GROUPS, 2, SIDE, TILE, PAD), f32),
            pltpu.VMEM((GROUPS, 2, SIDE, TILE, PAD), f32),
            pltpu.VMEM((GROUPS, 2 * SIDE, SIDE * TILE, PAD), f32),
            pltpu.VMEM((PAIRS, 2 * PAD, 2 * PAD), f32),
            pltpu.VMEM((PAIRS, 2 * PAD, 2 * PAD), bf16),
            pltpu.VMEM((PAIRS + 1, 2 * PAD, width), bf16),
            pltpu.VMEM((PAD, PAD), f32),
            pltpu.VMEM((PAD, PAD), f32),
            pltpu.VMEM((PAD, 2 * PAD), bf16),
            pltpu.VMEM((PAD, 2 * PAD), bf16),
            pltpu.VMEM((PAD, 2 * PAD), bf16),
            pltpu.SemaphoreType.DMA((2 * PAIRS,)),
            pltpu.SemaphoreType.DMA((GROUPS, 2, 2)),
            pltpu.SemaphoreType.DMA((GROUPS, 2, 6)),
            pltpu.SemaphoreType.DMA((6,)),
            pltpu.SemaphoreType.DMA((6,)),
        ],
        compiler_params=pltpu.CompilerParams(
            collective_id=0, has_side_effects=True, vmem_limit_bytes=58 * 2**20
        ),
    )(weight_delta)


def solution(mesh):
    return jax.shard_map(
        shards, mesh=mesh, in_specs=(P("col", "row"),), out_specs=P("col", "row"), check_vma=False
    )
```

```python
import functools

import jax
import jax.numpy as jnp
from jax import lax
from jax.experimental import pallas as pl
from jax.experimental.pallas import tpu as pltpu
from jax.sharding import PartitionSpec as P

BLOCK = 112
PAD = 128
PAIRS = 4
SIDE = 8
CHUNK = 56
SHORT = 48
STRIP = 16
TILE = 8
GROUPS = 3
EPS = 1e-6
STAGE, LAG, TURN = 10, 5, 60.5
CROSS_ORDER = (0, 3, 1, 2)
CROSS_PLACE = {0: (1, 0), 3: (1, 1), 1: (2, 0), 2: (2, 1)}
CHUNK_ROWS = {(0, 0): CHUNK, (0, 1): CHUNK, (1, 0): SHORT, (1, 1): CHUNK, (2, 0): SHORT, (2, 1): SHORT}
MESH = pl.DeviceIdType.MESH
FAR_FIRST = (4, 3, 5, 2, 6, 1, 7)


def dot(a, b):
    return jnp.dot(a, b, preferred_element_type=jnp.float32)


def dot_nt(a, b):
    return lax.dot_general(a, b, (((1,), (1,)), ((), ())), preferred_element_type=jnp.float32)


def halves(x):
    high = x.astype(jnp.bfloat16)
    low = (x - high.astype(jnp.float32)).astype(jnp.bfloat16)
    return high, low


def dot3(a, b):
    a_high, a_low = a
    b_high, b_low = b
    return dot(
        jnp.concatenate([a_high, a_high, a_low], axis=1), jnp.concatenate([b_high, b_low, b_high], axis=0)
    )


def both_sides(left, x, right):
    product = dot(jnp.concatenate([left, left], axis=1), jnp.concatenate(halves(x), axis=0))
    return dot_nt(jnp.concatenate(halves(product), axis=1), jnp.concatenate([right, right], axis=1))


def turning_transposed(gram):
    shape = gram.shape
    eye = lax.broadcasted_iota(jnp.int32, shape, 0) == lax.broadcasted_iota(jnp.int32, shape, 1)
    small_eye = eye[:PAD, :PAD]
    corners = [jnp.where(small_eye, gram[i : i + PAD, i : i + PAD], 0.0) for i in (0, PAD)]
    down = jnp.concatenate([jnp.sum(x, axis=1, keepdims=True) for x in corners], axis=0) + EPS
    across = jnp.concatenate([jnp.sum(x, axis=0, keepdims=True) for x in corners], axis=1) + EPS
    inverse_across = lax.rsqrt(across)
    normed = gram * lax.rsqrt(down) * inverse_across
    parts = halves(normed)
    square = dot3(parts, parts)
    bound = jnp.max(jnp.sum(jnp.abs(normed), axis=0, keepdims=True), axis=1, keepdims=True)
    share = 1.0 / bound
    share2 = share * share
    rest = dot3(halves(square), halves((-0.5625 * share * share2) * normed + (0.0625 * share2 * share2) * square))
    factor = jnp.where(eye, 2.25, 0.0) + (-2.4375 * share) * normed + (1.6875 * share2) * square + rest
    return (factor * (jnp.sqrt(down) * lax.rsqrt(bound)) * inverse_across).astype(jnp.bfloat16)


def tile_iotas():
    return (
        lax.broadcasted_iota(jnp.int32, (PAD, PAD), 0),
        lax.broadcasted_iota(jnp.int32, (PAD, PAD), 1),
    )


def packed(first, last):
    row, column = tile_iotas()
    turned = pltpu.roll(last, PAD - 1, 1)
    return jnp.where((column < row) | (column == PAD - 1), turned, first)[:BLOCK]


def padded(x):
    return jnp.concatenate([x, jnp.zeros((PAD - BLOCK, PAD), jnp.float32)], axis=0)


def unpacked(both):
    row, column = tile_iotas()
    both = padded(both)
    first = jnp.where((column >= row) & (column < BLOCK), both, 0.0)
    first = jnp.where(column >= row, first, first.T)
    last = jnp.where(column <= row, pltpu.roll(both, 1, 1), 0.0)
    last = jnp.where(column <= row, last, last.T)
    return first, last


def lanes(rows):
    return lax.broadcasted_iota(jnp.int32, (rows, PAD), 1)


def folded(x):
    quarters = [x[i : i + BLOCK, j : j + PAD] for i in (0, PAD) for j in (0, PAD)]
    kept = jnp.concatenate(quarters[:3] + [quarters[3][:SHORT]], axis=0)
    lower = quarters[3][SHORT:]
    strips = jnp.concatenate([pltpu.roll(lower, BLOCK - STRIP * i, 1) for i in range(BLOCK // STRIP)], axis=0)
    count = kept.shape[0]
    return jnp.where(lanes(count) < BLOCK, kept, strips[:count]), strips[count:]


def unfolded(kept, extra):
    strips = jnp.concatenate([kept, extra], axis=0)
    height = BLOCK - SHORT
    lane = lanes(height)
    lower = jnp.zeros((height, PAD), jnp.float32)
    for i in range(BLOCK // STRIP):
        moved = pltpu.roll(strips[i * height : (i + 1) * height], STRIP * (i + 1), 1)
        lower = jnp.where((lane >= STRIP * i) & (lane < STRIP * (i + 1)), moved, lower)
    kept = jnp.where(lanes(kept.shape[0]) < BLOCK, kept, 0.0)
    quarters = [kept[i * BLOCK : (i + 1) * BLOCK] for i in range(3)]
    return quarters + [jnp.concatenate([kept[3 * BLOCK :], lower], axis=0)]


def square_of(a, b, c, d):
    return jnp.concatenate([jnp.concatenate([a, b], axis=1), jnp.concatenate([c, d], axis=1)], axis=0)


def kernel(
    x_ref, o_ref, own, beside, part, relay_in, relay_out, final_in, middle, tiles, full, grams, turn, stack, corner,
    corner_in, turn_in, wide, wide_in, in_sem, send_sem, recv_sem, side_send, side_recv,
):
    c, r = lax.axis_index("col"), lax.axis_index("row")
    col_count = lax.axis_size("col")
    z, y = lax.div(r, SIDE), lax.rem(r, SIDE)
    left, right = (lax.rem(c + col_count - 1, col_count), r), (lax.rem(c + 1, col_count), r)
    tie = 2 * lax.rem(c, 2) - 1

    def ring(place, step):
        return lax.rem(place + step + SIDE, SIDE)

    def along_y(step):
        return (c, z * SIDE + ring(y, step))

    def along_z(step):
        return (c, ring(z, step) * SIDE + y)

    places = ((y, z), (z, y))
    movers = ((along_y, along_z), (along_z, along_y))

    barrier = pltpu.get_barrier_semaphore()
    for step in range(1, SIDE):
        pl.semaphore_signal(barrier, inc=1, device_id=along_y(step), device_id_type=MESH)
        pl.semaphore_signal(barrier, inc=1, device_id=along_z(step), device_id_type=MESH)
    for side in (left, right):
        pl.semaphore_signal(barrier, inc=1, device_id=side, device_id_type=MESH)

    loads = []
    for b in range(2 * PAIRS):
        loads.append(
            pltpu.make_async_copy(
                x_ref.at[pl.ds(b * BLOCK, BLOCK)], own.at[b // 2, pl.ds((b % 2) * PAD, BLOCK)], in_sem.at[b]
            )
        )
        loads[-1].start()
    gap = jnp.zeros((PAD - BLOCK, own.shape[-1]), jnp.bfloat16)
    for lower in (BLOCK, PAD + BLOCK):
        beside[pl.ds(lower, PAD - BLOCK)] = gap
        for k in range(PAIRS):
            own[k, pl.ds(lower, PAD - BLOCK)] = gap
    for group in range(GROUPS):
        for half in range(2):
            for tile in range(CHUNK_ROWS[group, half] // TILE, SIDE):
                middle[group, half, tile] = jnp.zeros((TILE, PAD), jnp.float32)

    def sideways(source, target, index, device):
        return pltpu.make_async_remote_copy(
            src_ref=source, dst_ref=target, send_sem=side_send.at[index], recv_sem=side_recv.at[index],
            device_id=device, device_id_type=MESH,
        )

    pair_out = [
        sideways(x_ref.at[pl.ds(b * BLOCK, BLOCK)], beside.at[pl.ds(b * PAD, BLOCK)], b, left) for b in range(2)
    ]
    turn_out = sideways(turn.at[0, pl.ds(PAD, PAD)], turn_in, 2, left)
    corner_out = sideways(corner, corner_in, 3, left)
    block_out = sideways(stack.at[PAIRS, pl.ds(0, PAD)], stack.at[0, pl.ds(0, PAD)], 4, right)
    wide_out = sideways(wide, wide_in, 5, right)

    def send(group, half, axis, step, source, target, kind, small=0):
        pltpu.make_async_remote_copy(
            src_ref=source, dst_ref=target, send_sem=send_sem.at[group, half, small],
            recv_sem=recv_sem.at[group, half, kind], device_id=movers[half][axis](step), device_id_type=MESH,
        ).start()

    def arrived(like, group, half, kind):
        pltpu.make_async_copy(like, like, recv_sem.at[group, half, kind]).wait()

    def chunk_of(ref, group, half, step):
        return ref.at[group, half * SIDE + ring(places[half][0], step), pl.ds(0, CHUNK_ROWS[group, half])]

    def slot_of(ref, group, half, slot):
        return ref.at[group, half, slot, pl.ds(0, CHUNK_ROWS[group, half])]

    def slots_of(ref, group, half, count):
        return ref.at[group, half, pl.ds(0, count), pl.ds(0, CHUNK_ROWS[group, half])]

    def spread(group, half):
        send(group, half, 0, 2 * tie, chunk_of(part, group, half, 4), slot_of(relay_in, group, half, 2), 0)
        for slot, step in enumerate((1, -1)):
            send(group, half, 0, step, chunk_of(part, group, half, 3 * step), slot_of(relay_in, group, half, slot), 0)

    def spread_near(group, half):
        for slot, step in enumerate((1, -1)):
            send(group, half, 0, step, chunk_of(part, group, half, step), slot_of(final_in, group, half, slot), 1)

    def relay(group, half):
        arrived(slots_of(relay_in, group, half, 3), group, half, 0)
        for slot, step in enumerate((1, -1)):
            here = chunk_of(part, group, half, 2 * step)[...] + slot_of(relay_in, group, half, slot)[...]
            out = slot_of(relay_out, group, half, slot)
            out[...] = here + jnp.where(tie == step, slot_of(relay_in, group, half, 2)[...], 0.0)
            send(group, half, 0, 2 * step, out, slot_of(final_in, group, half, 2 + slot), 1)

    def cross(group, half):
        arrived(slots_of(final_in, group, half, 4), group, half, 1)
        total = chunk_of(part, group, half, 0)[...]
        for slot in range(4):
            total = total + slot_of(final_in, group, half, slot)[...]
        count = CHUNK_ROWS[group, half] // TILE
        middle[group, half, pl.ds(0, count)] = total.reshape(count, TILE, PAD)
        place = places[half][1]
        for step in FAR_FIRST:
            send(
                group, half, 1, step, middle.at[group, half, ring(place, step)], tiles.at[group, half, place], 2, 1
            )
        tiles[group, half, place] = middle[group, half, place]

    def back(group, half):
        arrived(tiles.at[group, half, pl.ds(0, SIDE - 1)], group, half, 2)
        total = tiles[group, half, 0]
        for i in range(1, SIDE):
            total = total + tiles[group, half, i]
        first, second = places[half]
        here = full.at[group, half * SIDE + first, pl.ds(pl.multiple_of(second * TILE, TILE), TILE)]
        here[...] = total
        for step in FAR_FIRST:
            send(group, half, 1, step, here, here, 3, 1)

    def share(group, half):
        arrived(tiles.at[group, half, pl.ds(0, SIDE - 1)], group, half, 3)
        here = chunk_of(full, group, half, 0)
        for step in (2, -2):
            send(group, half, 0, step, here, here, 4)

    def share_near(group, half):
        here = chunk_of(full, group, half, 0)
        for step in (1, -1):
            send(group, half, 0, step, here, here, 5)

    def pass_on(group, half):
        arrived(slots_of(final_in, group, half, 2), group, half, 4)
        here = chunk_of(full, group, half, -2 * tie)
        send(group, half, 0, 2 * tie, here, here, 5)
        for step in (1, -1):
            here = chunk_of(full, group, half, -2 * step)
            send(group, half, 0, step, here, here, 5)

    def complete(group, half):
        arrived(full.at[group, pl.ds(0, 5), pl.ds(0, CHUNK_ROWS[group, half])], group, half, 5)

    def put(group, chunk, x):
        part[group, pl.ds(chunk, 2)] = x[:BLOCK].reshape(2, CHUNK, PAD)

    def take(group, chunk):
        return full[group, pl.ds(chunk, 2), pl.ds(0, CHUNK)].reshape(BLOCK, PAD)

    firsts, lasts, turnings = {}, {}, {}

    def gram_products():
        for copy in loads:
            copy.wait()
        for k in range(PAIRS):
            pair = own[k]
            gram = dot_nt(pair, pair)
            put(0, 4 * k, packed(gram[:PAD, :PAD], gram[PAD:, PAD:]))
            between = gram[:BLOCK, PAD:]
            if k < PAIRS - 1:
                kept, extra = folded(dot_nt(pair, own[k + 1]))
                group, half = CROSS_PLACE[k]
                part[group, pl.ds(half * SIDE, SIDE), pl.ds(0, SHORT)] = kept.reshape(SIDE, SHORT, PAD)
                rows = extra.shape[0]
                beginning = jnp.where(lanes(rows) < BLOCK, between[:rows], extra)
                between = jnp.concatenate([beginning, between[rows:]], axis=0)
            put(0, 4 * k + 2, between)

    def begin():
        pl.semaphore_wait(barrier, 2 * (SIDE - 1) + 2)
        for copy in pair_out:
            copy.start()
        for half in range(2):
            spread(0, half)

    def cross_products(k):
        group, half = CROSS_PLACE[k]
        if k == PAIRS - 1:
            for copy in pair_out:
                copy.wait_recv()
            gram = dot_nt(own[k], beside[...])
            put(group, half * SIDE, gram[:PAD, :PAD])
            put(group, half * SIDE + 2, gram[:PAD, PAD:])
            put(group, half * SIDE + 4, gram[PAD:, :PAD])
            put(group, half * SIDE + 6, gram[PAD:, PAD:])
        spread(group, half)

    def cross_quarters(k):
        group, half = CROSS_PLACE[k]
        if k == PAIRS - 1:
            return [padded(take(group, half * SIDE + 2 * i)) for i in range(4)]
        kept = full[group, pl.ds(half * SIDE, SIDE), pl.ds(0, SHORT)].reshape(SIDE * SHORT, PAD)
        return [padded(x) for x in unfolded(kept, take(0, 4 * k + 2)[: BLOCK - SHORT])]

    def first_turnings(*pairs):
        for k in pairs:
            first, last = unpacked(take(0, 4 * k))
            between = take(0, 4 * k + 2)
            between = padded(jnp.where(lanes(BLOCK) < BLOCK, between, 0.0))
            grams[k] = square_of(first, between, between.T, last)
        for k in pairs:
            turn[k] = turning_transposed(grams[k])
        if 0 in pairs:
            turn_out.start()

    def first_update(k):
        updated = dot(turn[k], own[k]).astype(jnp.bfloat16)
        stack[k + 1, pl.ds(0, PAD)] = updated[:PAD]
        stack[k, pl.ds(PAD, PAD)] = updated[PAD:]

    def turned_grams(*pairs):
        for k in pairs:
            lasts[k] = both_sides(turn[k, pl.ds(PAD, PAD)], grams[k], turn[k, pl.ds(PAD, PAD)])
        if 0 in pairs:
            corner[...] = lasts[0]
            corner_out.start()
        for k in pairs:
            firsts[k] = both_sides(turn[k, pl.ds(0, PAD)], grams[k], turn[k, pl.ds(0, PAD)])
        if PAIRS - 1 in pairs:
            first_update(PAIRS - 1)
            block_out.start()

    def first_updates():
        for k in range(PAIRS - 1):
            first_update(k)

    def update_beside():
        stack[PAIRS, pl.ds(PAD, PAD)] = dot(turn_in[...], beside[...]).astype(jnp.bfloat16)

    def second_turnings(*pairs):
        if PAIRS - 1 in pairs:
            turn_out.wait_recv()
            corner_out.wait_recv()
        between = {}
        for k in pairs:
            cross_gram = square_of(*cross_quarters(k))
            other = turn[k + 1, pl.ds(PAD, PAD)] if k < PAIRS - 1 else turn_in[...]
            between[k] = both_sides(turn[k, pl.ds(0, PAD)], cross_gram, other)
        for k in pairs:
            last = lasts[k + 1] if k < PAIRS - 1 else corner_in[...]
            turnings[k] = turning_transposed(square_of(firsts[k], between[k], between[k].T, last))
        if PAIRS - 1 in pairs:
            wide[...] = turnings[PAIRS - 1][:PAD]
            wide_out.start()
    def second_update(k):
        updated = dot(turnings[k], stack[k + 1]).astype(jnp.bfloat16)
        if k < PAIRS - 1:
            o_ref[pl.ds((2 * k + 1) * BLOCK, BLOCK)] = updated[PAD : PAD + BLOCK]
            o_ref[pl.ds((2 * k + 2) * BLOCK, BLOCK)] = updated[:BLOCK]
        else:
            o_ref[pl.ds((2 * k + 1) * BLOCK, BLOCK)] = jnp.where(c == col_count - 1, stack[PAIRS, pl.ds(0, BLOCK)], updated[PAD : PAD + BLOCK])

    def first_block():
        block_out.wait_recv()
        wide_out.wait_recv()
        updated = dot(wide_in[...], stack[0]).astype(jnp.bfloat16)[:BLOCK]
        o_ref[pl.ds(0, BLOCK)] = jnp.where(c == 0, stack[0, pl.ds(PAD, BLOCK)], updated)

    plan = [(0, gram_products), (0, begin)]
    plan += [(LAG, cross_products, k) for k in (0, 1, 3, 2)]
    units = [(0, 0), (0, 1)] + [CROSS_PLACE[k] for k in CROSS_ORDER]
    for i, unit in enumerate(units):
        for j, stage in enumerate((relay, cross, back, share, pass_on, complete)):
            plan.append(((j + 1) * STAGE + (LAG if i >= 2 else 0), stage, *unit))
    plan.append((54.9, complete, 0, 0))
    plan.append((54.9, first_turnings, 0))
    plan.append((54.9, turned_grams, 0))
    plan += [(LAG + 0.5, spread_near, *unit) for unit in units]
    plan += [(4 * STAGE + LAG + 0.5, share_near, *unit) for unit in units]
    plan.append((TURN, first_turnings, 1, 2, 3))
    plan.append((TURN, turned_grams, 1, 2, 3))
    plan.append((64.5, complete, *CROSS_PLACE[3]))
    plan.append((64.5, second_turnings, 3))
    plan.append((100, second_turnings, 0, 1, 2))
    plan.append((100, first_updates))
    plan.append((100, update_beside))
    plan += [(100, second_update, k) for k in range(PAIRS)]
    plan.append((100, first_block))
    plan.remove((6 * STAGE, complete, 0, 0))
    plan.remove((6 * STAGE + LAG, complete, *CROSS_PLACE[3]))
    for _, step, *where in sorted(plan, key=lambda entry: entry[0]):
        step(*where)

    for copy in pair_out + [turn_out, corner_out, block_out, wide_out]:
        copy.wait_send()
    for group in range(GROUPS):
        for half in range(2):
            for small, like in enumerate((full.at[group, pl.ds(0, 14), pl.ds(0, CHUNK_ROWS[group, half])], part.at[group, pl.ds(0, 2)])):
                pltpu.make_async_copy(like, like, send_sem.at[group, half, small]).wait()


def shards(weight_delta):
    width = weight_delta.shape[1]
    chunks = lambda count: pltpu.VMEM((GROUPS, 2, count, CHUNK, PAD), f32)
    f32, bf16 = jnp.float32, jnp.bfloat16
    return pl.pallas_call(
        kernel,
        out_shape=pltpu.VMEM(weight_delta.shape, bf16),
        in_specs=[pl.BlockSpec(memory_space=pl.ANY)],
        out_specs=pl.BlockSpec(memory_space=pltpu.VMEM),
        scratch_shapes=[
            pltpu.VMEM((PAIRS, 2 * PAD, width), bf16),
            pltpu.VMEM((2 * PAD, width), bf16),
            pltpu.VMEM((GROUPS, 2 * SIDE, CHUNK, PAD), f32),
            chunks(3),
            chunks(2),
            chunks(4),
            pltpu.VMEM((GROUPS, 2, SIDE, TILE, PAD), f32),
            pltpu.VMEM((GROUPS, 2, SIDE, TILE, PAD), f32),
            pltpu.VMEM((GROUPS, 2 * SIDE, SIDE * TILE, PAD), f32),
            pltpu.VMEM((PAIRS, 2 * PAD, 2 * PAD), f32),
            pltpu.VMEM((PAIRS, 2 * PAD, 2 * PAD), bf16),
            pltpu.VMEM((PAIRS + 1, 2 * PAD, width), bf16),
            pltpu.VMEM((PAD, PAD), f32),
            pltpu.VMEM((PAD, PAD), f32),
            pltpu.VMEM((PAD, 2 * PAD), bf16),
            pltpu.VMEM((PAD, 2 * PAD), bf16),
            pltpu.VMEM((PAD, 2 * PAD), bf16),
            pltpu.SemaphoreType.DMA((2 * PAIRS,)),
            pltpu.SemaphoreType.DMA((GROUPS, 2, 2)),
            pltpu.SemaphoreType.DMA((GROUPS, 2, 6)),
            pltpu.SemaphoreType.DMA((6,)),
            pltpu.SemaphoreType.DMA((6,)),
        ],
        compiler_params=pltpu.CompilerParams(
            collective_id=0, has_side_effects=True, vmem_limit_bytes=58 * 2**20
        ),
    )(weight_delta)


def solution(mesh):
    return jax.shard_map(
        shards, mesh=mesh, in_specs=(P("col", "row"),), out_specs=P("col", "row"), check_vma=False
    )
```

```python
import functools

import jax
import jax.numpy as jnp
from jax import lax
from jax.experimental import pallas as pl
from jax.experimental.pallas import tpu as pltpu
from jax.sharding import PartitionSpec as P

BLOCK = 112
PAD = 128
PAIRS = 4
SIDE = 8
CHUNK = 56
SHORT = 48
STRIP = 16
TILE = 8
GROUPS = 3
EPS = 1e-6
STAGE, LAG, TURN = 10, 5, 60.5
CROSS_ORDER = (0, 3, 1, 2)
CROSS_PLACE = {0: (1, 0), 3: (1, 1), 1: (2, 0), 2: (2, 1)}
CHUNK_ROWS = {(0, 0): CHUNK, (0, 1): CHUNK, (1, 0): SHORT, (1, 1): CHUNK, (2, 0): SHORT, (2, 1): SHORT}
MESH = pl.DeviceIdType.MESH
FAR_FIRST = (4, 3, 5, 2, 6, 1, 7)
NEAR = (1, -1, 2, -2)


def dot(a, b):
    return jnp.dot(a, b, preferred_element_type=jnp.float32)


def dot_nt(a, b):
    return lax.dot_general(a, b, (((1,), (1,)), ((), ())), preferred_element_type=jnp.float32)


def halves(x):
    high = x.astype(jnp.bfloat16)
    low = (x - high.astype(jnp.float32)).astype(jnp.bfloat16)
    return high, low


def dot3(a, b):
    a_high, a_low = a
    b_high, b_low = b
    return dot(
        jnp.concatenate([a_high, a_high, a_low], axis=1), jnp.concatenate([b_high, b_low, b_high], axis=0)
    )


def both_sides(left, x, right):
    product = dot(jnp.concatenate([left, left], axis=1), jnp.concatenate(halves(x), axis=0))
    return dot_nt(jnp.concatenate(halves(product), axis=1), jnp.concatenate([right, right], axis=1))


def turning_transposed(gram):
    shape = gram.shape
    eye = lax.broadcasted_iota(jnp.int32, shape, 0) == lax.broadcasted_iota(jnp.int32, shape, 1)
    small_eye = eye[:PAD, :PAD]
    corners = [jnp.where(small_eye, gram[i : i + PAD, i : i + PAD], 0.0) for i in (0, PAD)]
    down = jnp.concatenate([jnp.sum(x, axis=1, keepdims=True) for x in corners], axis=0) + EPS
    across = jnp.concatenate([jnp.sum(x, axis=0, keepdims=True) for x in corners], axis=1) + EPS
    inverse_across = lax.rsqrt(across)
    normed = gram * lax.rsqrt(down) * inverse_across
    parts = halves(normed)
    square = dot3(parts, parts)
    bound = jnp.max(jnp.sum(jnp.abs(normed), axis=0, keepdims=True), axis=1, keepdims=True)
    share = 1.0 / bound
    share2 = share * share
    rest = dot3(halves(square), halves((-0.5625 * share * share2) * normed + (0.0625 * share2 * share2) * square))
    factor = jnp.where(eye, 2.25, 0.0) + (-2.4375 * share) * normed + (1.6875 * share2) * square + rest
    return (factor * (jnp.sqrt(down) * lax.rsqrt(bound)) * inverse_across).astype(jnp.bfloat16)


def tile_iotas():
    return (
        lax.broadcasted_iota(jnp.int32, (PAD, PAD), 0),
        lax.broadcasted_iota(jnp.int32, (PAD, PAD), 1),
    )


def packed(first, last):
    row, column = tile_iotas()
    turned = pltpu.roll(last, PAD - 1, 1)
    return jnp.where((column < row) | (column == PAD - 1), turned, first)[:BLOCK]


def padded(x):
    return jnp.concatenate([x, jnp.zeros((PAD - BLOCK, PAD), jnp.float32)], axis=0)


def unpacked(both):
    row, column = tile_iotas()
    both = padded(both)
    first = jnp.where((column >= row) & (column < BLOCK), both, 0.0)
    first = jnp.where(column >= row, first, first.T)
    last = jnp.where(column <= row, pltpu.roll(both, 1, 1), 0.0)
    last = jnp.where(column <= row, last, last.T)
    return first, last


def lanes(rows):
    return lax.broadcasted_iota(jnp.int32, (rows, PAD), 1)


def folded(x):
    quarters = [x[i : i + BLOCK, j : j + PAD] for i in (0, PAD) for j in (0, PAD)]
    kept = jnp.concatenate(quarters[:3] + [quarters[3][:SHORT]], axis=0)
    lower = quarters[3][SHORT:]
    strips = jnp.concatenate([pltpu.roll(lower, BLOCK - STRIP * i, 1) for i in range(BLOCK // STRIP)], axis=0)
    count = kept.shape[0]
    return jnp.where(lanes(count) < BLOCK, kept, strips[:count]), strips[count:]


def unfolded(kept, extra):
    strips = jnp.concatenate([kept, extra], axis=0)
    height = BLOCK - SHORT
    lane = lanes(height)
    lower = jnp.zeros((height, PAD), jnp.float32)
    for i in range(BLOCK // STRIP):
        moved = pltpu.roll(strips[i * height : (i + 1) * height], STRIP * (i + 1), 1)
        lower = jnp.where((lane >= STRIP * i) & (lane < STRIP * (i + 1)), moved, lower)
    kept = jnp.where(lanes(kept.shape[0]) < BLOCK, kept, 0.0)
    quarters = [kept[i * BLOCK : (i + 1) * BLOCK] for i in range(3)]
    return quarters + [jnp.concatenate([kept[3 * BLOCK :], lower], axis=0)]


def square_of(a, b, c, d):
    return jnp.concatenate([jnp.concatenate([a, b], axis=1), jnp.concatenate([c, d], axis=1)], axis=0)


def kernel(
    x_ref, o_ref, own, beside, part, relay_in, relay_out, final_in, middle, tiles, full, grams, turn, stack, corner,
    corner_in, turn_in, wide, wide_in, in_sem, send_sem, recv_sem, side_send, side_recv,
):
    c, r = lax.axis_index("col"), lax.axis_index("row")
    col_count = lax.axis_size("col")
    z, y = lax.div(r, SIDE), lax.rem(r, SIDE)
    left, right = (lax.rem(c + col_count - 1, col_count), r), (lax.rem(c + 1, col_count), r)
    tie = 2 * lax.rem(c, 2) - 1

    def ring(place, step):
        return lax.rem(place + step + SIDE, SIDE)

    def along_y(step):
        return (c, z * SIDE + ring(y, step))

    def along_z(step):
        return (c, ring(z, step) * SIDE + y)

    places = ((y, z), (z, y))
    movers = ((along_y, along_z), (along_z, along_y))

    barrier = pltpu.get_barrier_semaphore()
    for step in NEAR:
        pl.semaphore_signal(barrier, inc=1, device_id=along_y(step), device_id_type=MESH)
        pl.semaphore_signal(barrier, inc=1, device_id=along_z(step), device_id_type=MESH)
    for side in (left, right):
        pl.semaphore_signal(barrier, inc=1, device_id=side, device_id_type=MESH)

    loads = []
    for b in range(2 * PAIRS):
        loads.append(
            pltpu.make_async_copy(
                x_ref.at[pl.ds(b * BLOCK, BLOCK)], own.at[b // 2, pl.ds((b % 2) * PAD, BLOCK)], in_sem.at[b]
            )
        )
        loads[-1].start()
    gap = jnp.zeros((PAD - BLOCK, own.shape[-1]), jnp.bfloat16)
    for lower in (BLOCK, PAD + BLOCK):
        beside[pl.ds(lower, PAD - BLOCK)] = gap
        for k in range(PAIRS):
            own[k, pl.ds(lower, PAD - BLOCK)] = gap
    for group in range(GROUPS):
        for half in range(2):
            for tile in range(CHUNK_ROWS[group, half] // TILE, SIDE):
                middle[group, half, tile] = jnp.zeros((TILE, PAD), jnp.float32)

    def sideways(source, target, index, device):
        return pltpu.make_async_remote_copy(
            src_ref=source, dst_ref=target, send_sem=side_send.at[index], recv_sem=side_recv.at[index],
            device_id=device, device_id_type=MESH,
        )

    pair_out = [
        sideways(x_ref.at[pl.ds(b * BLOCK, BLOCK)], beside.at[pl.ds(b * PAD, BLOCK)], b, left) for b in range(2)
    ]
    turn_out = sideways(turn.at[0, pl.ds(PAD, PAD)], turn_in, 2, left)
    corner_out = sideways(corner, corner_in, 3, left)
    block_out = sideways(stack.at[PAIRS, pl.ds(0, PAD)], stack.at[0, pl.ds(0, PAD)], 4, right)
    wide_out = sideways(wide, wide_in, 5, right)

    def send(group, half, axis, step, source, target, kind, small=0):
        pltpu.make_async_remote_copy(
            src_ref=source, dst_ref=target, send_sem=send_sem.at[group, half, small],
            recv_sem=recv_sem.at[group, half, kind], device_id=movers[half][axis](step), device_id_type=MESH,
        ).start()

    def arrived(like, group, half, kind):
        pltpu.make_async_copy(like, like, recv_sem.at[group, half, kind]).wait()

    def chunk_of(ref, group, half, step):
        return ref.at[group, half * SIDE + ring(places[half][0], step), pl.ds(0, CHUNK_ROWS[group, half])]

    def slot_of(ref, group, half, slot):
        return ref.at[group, half, slot, pl.ds(0, CHUNK_ROWS[group, half])]

    def slots_of(ref, group, half, count):
        return ref.at[group, half, pl.ds(0, count), pl.ds(0, CHUNK_ROWS[group, half])]

    def spread(group, half):
        send(group, half, 0, 2 * tie, chunk_of(part, group, half, 4), slot_of(relay_in, group, half, 2), 0)
        for slot, step in enumerate((1, -1)):
            send(group, half, 0, step, chunk_of(part, group, half, 3 * step), slot_of(relay_in, group, half, slot), 0)

    def spread_near(group, half):
        for slot, step in enumerate((1, -1)):
            send(group, half, 0, step, chunk_of(part, group, half, step), slot_of(final_in, group, half, slot), 1)

    def relay(group, half):
        arrived(slots_of(relay_in, group, half, 3), group, half, 0)
        for slot, step in enumerate((1, -1)):
            here = chunk_of(part, group, half, 2 * step)[...] + slot_of(relay_in, group, half, slot)[...]
            out = slot_of(relay_out, group, half, slot)
            out[...] = here + jnp.where(tie == step, slot_of(relay_in, group, half, 2)[...], 0.0)
            send(group, half, 0, 2 * step, out, slot_of(final_in, group, half, 2 + slot), 1)

    def met():
        for half in range(2):
            arrived(slots_of(final_in, 0, half, 4), 0, half, 1)

    def cross(group, half):
        if group > 0:
            arrived(slots_of(final_in, group, half, 4), group, half, 1)
        total = chunk_of(part, group, half, 0)[...]
        for slot in range(4):
            total = total + slot_of(final_in, group, half, slot)[...]
        count = CHUNK_ROWS[group, half] // TILE
        middle[group, half, pl.ds(0, count)] = total.reshape(count, TILE, PAD)
        place = places[half][1]
        for step in FAR_FIRST:
            send(
                group, half, 1, step, middle.at[group, half, ring(place, step)], tiles.at[group, half, place], 2, 1
            )
        tiles[group, half, place] = middle[group, half, place]

    def back(group, half):
        arrived(tiles.at[group, half, pl.ds(0, SIDE - 1)], group, half, 2)
        total = tiles[group, half, 0]
        for i in range(1, SIDE):
            total = total + tiles[group, half, i]
        first, second = places[half]
        here = full.at[group, half * SIDE + first, pl.ds(pl.multiple_of(second * TILE, TILE), TILE)]
        here[...] = total
        for step in FAR_FIRST:
            send(group, half, 1, step, here, here, 3, 1)

    def share(group, half):
        arrived(tiles.at[group, half, pl.ds(0, SIDE - 1)], group, half, 3)
        here = chunk_of(full, group, half, 0)
        for step in (2, -2):
            send(group, half, 0, step, here, here, 4)

    def share_near(group, half):
        here = chunk_of(full, group, half, 0)
        for step in (1, -1):
            send(group, half, 0, step, here, here, 5)

    def pass_on(group, half):
        arrived(slots_of(final_in, group, half, 2), group, half, 4)
        here = chunk_of(full, group, half, -2 * tie)
        send(group, half, 0, 2 * tie, here, here, 5)
        for step in (1, -1):
            here = chunk_of(full, group, half, -2 * step)
            send(group, half, 0, step, here, here, 5)

    def complete(group, half):
        arrived(full.at[group, pl.ds(0, 5), pl.ds(0, CHUNK_ROWS[group, half])], group, half, 5)

    def put(group, chunk, x):
        part[group, pl.ds(chunk, 2)] = x[:BLOCK].reshape(2, CHUNK, PAD)

    def take(group, chunk):
        return full[group, pl.ds(chunk, 2), pl.ds(0, CHUNK)].reshape(BLOCK, PAD)

    firsts, lasts, turnings = {}, {}, {}

    def gram_products():
        for k in range(PAIRS):
            for b in range(2 * k + 2 if k else 0, min(2 * k + 4, 2 * PAIRS)):
                loads[b].wait()
            pair = own[k]
            gram = dot_nt(pair, pair)
            put(0, 4 * k, packed(gram[:PAD, :PAD], gram[PAD:, PAD:]))
            between = gram[:BLOCK, PAD:]
            if k < PAIRS - 1:
                kept, extra = folded(dot_nt(pair, own[k + 1]))
                group, half = CROSS_PLACE[k]
                part[group, pl.ds(half * SIDE, SIDE), pl.ds(0, SHORT)] = kept.reshape(SIDE, SHORT, PAD)
                rows = extra.shape[0]
                beginning = jnp.where(lanes(rows) < BLOCK, between[:rows], extra)
                between = jnp.concatenate([beginning, between[rows:]], axis=0)
            put(0, 4 * k + 2, between)

    def begin():
        pl.semaphore_wait(barrier, 2 * len(NEAR) + 2)
        for copy in pair_out:
            copy.start()
        for half in range(2):
            spread(0, half)

    def cross_products(k):
        group, half = CROSS_PLACE[k]
        if k == PAIRS - 1:
            for copy in pair_out:
                copy.wait_recv()
            gram = dot_nt(own[k], beside[...])
            put(group, half * SIDE, gram[:PAD, :PAD])
            put(group, half * SIDE + 2, gram[:PAD, PAD:])
            put(group, half * SIDE + 4, gram[PAD:, :PAD])
            put(group, half * SIDE + 6, gram[PAD:, PAD:])
        spread(group, half)

    def cross_quarters(k):
        group, half = CROSS_PLACE[k]
        if k == PAIRS - 1:
            return [padded(take(group, half * SIDE + 2 * i)) for i in range(4)]
        kept = full[group, pl.ds(half * SIDE, SIDE), pl.ds(0, SHORT)].reshape(SIDE * SHORT, PAD)
        return [padded(x) for x in unfolded(kept, take(0, 4 * k + 2)[: BLOCK - SHORT])]

    def first_turnings(*pairs):
        for k in pairs:
            first, last = unpacked(take(0, 4 * k))
            between = take(0, 4 * k + 2)
            between = padded(jnp.where(lanes(BLOCK) < BLOCK, between, 0.0))
            grams[k] = square_of(first, between, between.T, last)
        for k in pairs:
            turn[k] = turning_transposed(grams[k])
        if 0 in pairs:
            turn_out.start()

    def first_update(k):
        updated = dot(turn[k], own[k]).astype(jnp.bfloat16)
        stack[k + 1, pl.ds(0, PAD)] = updated[:PAD]
        stack[k, pl.ds(PAD, PAD)] = updated[PAD:]

    def turned_grams(*pairs):
        for k in pairs:
            lasts[k] = both_sides(turn[k, pl.ds(PAD, PAD)], grams[k], turn[k, pl.ds(PAD, PAD)])
        if 0 in pairs:
            corner[...] = lasts[0]
            corner_out.start()
        for k in pairs:
            firsts[k] = both_sides(turn[k, pl.ds(0, PAD)], grams[k], turn[k, pl.ds(0, PAD)])
        if PAIRS - 1 in pairs:
            first_update(PAIRS - 1)
            block_out.start()

    def first_updates():
        for k in range(PAIRS - 1):
            first_update(k)

    def update_beside():
        stack[PAIRS, pl.ds(PAD, PAD)] = dot(turn_in[...], beside[...]).astype(jnp.bfloat16)

    def second_turnings(*pairs):
        if PAIRS - 1 in pairs:
            turn_out.wait_recv()
            corner_out.wait_recv()
        between = {}
        for k in pairs:
            cross_gram = square_of(*cross_quarters(k))
            other = turn[k + 1, pl.ds(PAD, PAD)] if k < PAIRS - 1 else turn_in[...]
            between[k] = both_sides(turn[k, pl.ds(0, PAD)], cross_gram, other)
        for k in pairs:
            last = lasts[k + 1] if k < PAIRS - 1 else corner_in[...]
            turnings[k] = turning_transposed(square_of(firsts[k], between[k], between[k].T, last))
        if PAIRS - 1 in pairs:
            wide[...] = turnings[PAIRS - 1][:PAD]
            wide_out.start()
    def second_update(k):
        updated = dot(turnings[k], stack[k + 1]).astype(jnp.bfloat16)
        if k < PAIRS - 1:
            o_ref[pl.ds((2 * k + 1) * BLOCK, BLOCK)] = updated[PAD : PAD + BLOCK]
            o_ref[pl.ds((2 * k + 2) * BLOCK, BLOCK)] = updated[:BLOCK]
        else:
            o_ref[pl.ds((2 * k + 1) * BLOCK, BLOCK)] = jnp.where(c == col_count - 1, stack[PAIRS, pl.ds(0, BLOCK)], updated[PAD : PAD + BLOCK])

    def first_block():
        block_out.wait_recv()
        wide_out.wait_recv()
        updated = dot(wide_in[...], stack[0]).astype(jnp.bfloat16)[:BLOCK]
        o_ref[pl.ds(0, BLOCK)] = jnp.where(c == 0, stack[0, pl.ds(PAD, BLOCK)], updated)

    plan = [(0, gram_products), (0, begin)]
    plan += [(LAG, cross_products, k) for k in (0, 1, 3, 2)]
    units = [(0, 0), (0, 1)] + [CROSS_PLACE[k] for k in CROSS_ORDER]
    for i, unit in enumerate(units):
        for j, stage in enumerate((relay, cross, back, share, pass_on, complete)):
            plan.append(((j + 1) * STAGE + (LAG if i >= 2 else 0), stage, *unit))
    plan.append((54.9, complete, 0, 0))
    plan.append((54.9, first_turnings, 0))
    plan.append((54.9, turned_grams, 0))
    plan += [(LAG + 0.5, spread_near, *unit) for unit in units]
    plan += [(4 * STAGE + LAG + 0.5, share_near, *unit) for unit in units]
    plan.append((2 * STAGE - 0.01, met))
    plan.append((TURN, first_turnings, 1, 2, 3))
    plan.append((TURN, turned_grams, 1, 2, 3))
    plan.append((64.5, complete, *CROSS_PLACE[3]))
    plan.append((64.5, second_turnings, 3))
    plan.append((100, second_turnings, 0, 1, 2))
    plan.append((100, first_updates))
    plan.append((100, update_beside))
    plan += [(100, second_update, k) for k in range(PAIRS)]
    plan.append((100, first_block))
    plan.remove((6 * STAGE, complete, 0, 0))
    plan.remove((6 * STAGE + LAG, complete, *CROSS_PLACE[3]))
    for _, step, *where in sorted(plan, key=lambda entry: entry[0]):
        step(*where)

    for copy in pair_out + [turn_out, corner_out, block_out, wide_out]:
        copy.wait_send()
    for group in range(GROUPS):
        for half in range(2):
            for small, like in enumerate((full.at[group, pl.ds(0, 14), pl.ds(0, CHUNK_ROWS[group, half])], part.at[group, pl.ds(0, 2)])):
                pltpu.make_async_copy(like, like, send_sem.at[group, half, small]).wait()


def shards(weight_delta):
    width = weight_delta.shape[1]
    chunks = lambda count: pltpu.VMEM((GROUPS, 2, count, CHUNK, PAD), f32)
    f32, bf16 = jnp.float32, jnp.bfloat16
    return pl.pallas_call(
        kernel,
        out_shape=pltpu.VMEM(weight_delta.shape, bf16),
        in_specs=[pl.BlockSpec(memory_space=pl.ANY)],
        out_specs=pl.BlockSpec(memory_space=pltpu.VMEM),
        scratch_shapes=[
            pltpu.VMEM((PAIRS, 2 * PAD, width), bf16),
            pltpu.VMEM((2 * PAD, width), bf16),
            pltpu.VMEM((GROUPS, 2 * SIDE, CHUNK, PAD), f32),
            chunks(3),
            chunks(2),
            chunks(4),
            pltpu.VMEM((GROUPS, 2, SIDE, TILE, PAD), f32),
            pltpu.VMEM((GROUPS, 2, SIDE, TILE, PAD), f32),
            pltpu.VMEM((GROUPS, 2 * SIDE, SIDE * TILE, PAD), f32),
            pltpu.VMEM((PAIRS, 2 * PAD, 2 * PAD), f32),
            pltpu.VMEM((PAIRS, 2 * PAD, 2 * PAD), bf16),
            pltpu.VMEM((PAIRS + 1, 2 * PAD, width), bf16),
            pltpu.VMEM((PAD, PAD), f32),
            pltpu.VMEM((PAD, PAD), f32),
            pltpu.VMEM((PAD, 2 * PAD), bf16),
            pltpu.VMEM((PAD, 2 * PAD), bf16),
            pltpu.VMEM((PAD, 2 * PAD), bf16),
            pltpu.SemaphoreType.DMA((2 * PAIRS,)),
            pltpu.SemaphoreType.DMA((GROUPS, 2, 2)),
            pltpu.SemaphoreType.DMA((GROUPS, 2, 6)),
            pltpu.SemaphoreType.DMA((6,)),
            pltpu.SemaphoreType.DMA((6,)),
        ],
        compiler_params=pltpu.CompilerParams(
            collective_id=0, has_side_effects=True, vmem_limit_bytes=58 * 2**20
        ),
    )(weight_delta)


def solution(mesh):
    return jax.shard_map(
        shards, mesh=mesh, in_specs=(P("col", "row"),), out_specs=P("col", "row"), check_vma=False
    )
```

```python
import functools

import jax
import jax.numpy as jnp
from jax import lax
from jax.experimental import pallas as pl
from jax.experimental.pallas import tpu as pltpu
from jax.sharding import PartitionSpec as P

BLOCK = 112
PAD = 128
PAIRS = 4
SIDE = 8
CHUNK = 56
SHORT = 48
STRIP = 16
TILE = 8
GROUPS = 3
EPS = 1e-6
STAGE, LAG, TURN = 10, 5, 60.5
CROSS_ORDER = (0, 3, 1, 2)
CROSS_PLACE = {0: (1, 0), 3: (1, 1), 1: (2, 0), 2: (2, 1)}
CHUNK_ROWS = {(0, 0): CHUNK, (0, 1): CHUNK, (1, 0): SHORT, (1, 1): CHUNK, (2, 0): SHORT, (2, 1): SHORT}
MESH = pl.DeviceIdType.MESH
FAR_FIRST = (4, 3, 5, 2, 6, 1, 7)
NEAR = (1, -1, 2, -2)


def dot(a, b):
    return jnp.dot(a, b, preferred_element_type=jnp.float32)


def dot_nt(a, b):
    return lax.dot_general(a, b, (((1,), (1,)), ((), ())), preferred_element_type=jnp.float32)


def halves(x):
    high = x.astype(jnp.bfloat16)
    low = (x - high.astype(jnp.float32)).astype(jnp.bfloat16)
    return high, low


def dot3(a, b):
    a_high, a_low = a
    b_high, b_low = b
    return dot(
        jnp.concatenate([a_high, a_high, a_low], axis=1), jnp.concatenate([b_high, b_low, b_high], axis=0)
    )


def both_sides(left, x, right):
    product = dot(jnp.concatenate([left, left], axis=1), jnp.concatenate(halves(x), axis=0))
    return dot_nt(jnp.concatenate(halves(product), axis=1), jnp.concatenate([right, right], axis=1))


def turning_transposed(gram):
    shape = gram.shape
    eye = lax.broadcasted_iota(jnp.int32, shape, 0) == lax.broadcasted_iota(jnp.int32, shape, 1)
    small_eye = eye[:PAD, :PAD]
    corners = [jnp.where(small_eye, gram[i : i + PAD, i : i + PAD], 0.0) for i in (0, PAD)]
    down = jnp.concatenate([jnp.sum(x, axis=1, keepdims=True) for x in corners], axis=0) + EPS
    across = jnp.concatenate([jnp.sum(x, axis=0, keepdims=True) for x in corners], axis=1) + EPS
    inverse_across = lax.rsqrt(across)
    normed = gram * lax.rsqrt(down) * inverse_across
    parts = halves(normed)
    square = dot3(parts, parts)
    bound = jnp.max(jnp.sum(jnp.abs(normed), axis=0, keepdims=True), axis=1, keepdims=True)
    share = 1.0 / bound
    share2 = share * share
    rest = dot3(halves(square), halves((-0.5625 * share * share2) * normed + (0.0625 * share2 * share2) * square))
    factor = jnp.where(eye, 2.25, 0.0) + (-2.4375 * share) * normed + (1.6875 * share2) * square + rest
    return (factor * (jnp.sqrt(down) * lax.rsqrt(bound)) * inverse_across).astype(jnp.bfloat16)


def tile_iotas():
    return (
        lax.broadcasted_iota(jnp.int32, (PAD, PAD), 0),
        lax.broadcasted_iota(jnp.int32, (PAD, PAD), 1),
    )


def packed(first, last):
    row, column = tile_iotas()
    turned = pltpu.roll(last, PAD - 1, 1)
    return jnp.where((column < row) | (column == PAD - 1), turned, first)[:BLOCK]


def padded(x):
    return jnp.concatenate([x, jnp.zeros((PAD - BLOCK, PAD), jnp.float32)], axis=0)


def unpacked(both):
    row, column = tile_iotas()
    both = padded(both)
    first = jnp.where((column >= row) & (column < BLOCK), both, 0.0)
    first = jnp.where(column >= row, first, first.T)
    last = jnp.where(column <= row, pltpu.roll(both, 1, 1), 0.0)
    last = jnp.where(column <= row, last, last.T)
    return first, last


def lanes(rows):
    return lax.broadcasted_iota(jnp.int32, (rows, PAD), 1)


def folded(x):
    quarters = [x[i : i + BLOCK, j : j + PAD] for i in (0, PAD) for j in (0, PAD)]
    kept = jnp.concatenate(quarters[:3] + [quarters[3][:SHORT]], axis=0)
    lower = quarters[3][SHORT:]
    strips = jnp.concatenate([pltpu.roll(lower, BLOCK - STRIP * i, 1) for i in range(BLOCK // STRIP)], axis=0)
    count = kept.shape[0]
    return jnp.where(lanes(count) < BLOCK, kept, strips[:count]), strips[count:]


def unfolded(kept, extra):
    strips = jnp.concatenate([kept, extra], axis=0)
    height = BLOCK - SHORT
    lane = lanes(height)
    lower = jnp.zeros((height, PAD), jnp.float32)
    for i in range(BLOCK // STRIP):
        moved = pltpu.roll(strips[i * height : (i + 1) * height], STRIP * (i + 1), 1)
        lower = jnp.where((lane >= STRIP * i) & (lane < STRIP * (i + 1)), moved, lower)
    kept = jnp.where(lanes(kept.shape[0]) < BLOCK, kept, 0.0)
    quarters = [kept[i * BLOCK : (i + 1) * BLOCK] for i in range(3)]
    return quarters + [jnp.concatenate([kept[3 * BLOCK :], lower], axis=0)]


def square_of(a, b, c, d):
    return jnp.concatenate([jnp.concatenate([a, b], axis=1), jnp.concatenate([c, d], axis=1)], axis=0)


def kernel(
    x_ref, o_ref, own, beside, part, relay_in, relay_out, final_in, middle, tiles, full, grams, turn, stack, corner,
    corner_in, turn_in, wide, wide_in, in_sem, send_sem, recv_sem, side_send, side_recv,
):
    c, r = lax.axis_index("col"), lax.axis_index("row")
    col_count = lax.axis_size("col")
    z, y = lax.div(r, SIDE), lax.rem(r, SIDE)
    left, right = (lax.rem(c + col_count - 1, col_count), r), (lax.rem(c + 1, col_count), r)
    tie = 2 * lax.rem(c, 2) - 1

    def ring(place, step):
        return lax.rem(place + step + SIDE, SIDE)

    def along_y(step):
        return (c, z * SIDE + ring(y, step))

    def along_z(step):
        return (c, ring(z, step) * SIDE + y)

    places = ((y, z), (z, y))
    movers = ((along_y, along_z), (along_z, along_y))

    barrier = pltpu.get_barrier_semaphore()
    for step in NEAR:
        pl.semaphore_signal(barrier, inc=1, device_id=along_y(step), device_id_type=MESH)
        pl.semaphore_signal(barrier, inc=1, device_id=along_z(step), device_id_type=MESH)
    for side in (left, right):
        pl.semaphore_signal(barrier, inc=1, device_id=side, device_id_type=MESH)

    loads = []
    for b in range(2 * PAIRS):
        loads.append(
            pltpu.make_async_copy(
                x_ref.at[pl.ds(b * BLOCK, BLOCK)], own.at[b // 2, pl.ds((b % 2) * PAD, BLOCK)], in_sem.at[b]
            )
        )
        loads[-1].start()
    gap = jnp.zeros((PAD - BLOCK, own.shape[-1]), jnp.bfloat16)
    for lower in (BLOCK, PAD + BLOCK):
        beside[pl.ds(lower, PAD - BLOCK)] = gap
        for k in range(PAIRS):
            own[k, pl.ds(lower, PAD - BLOCK)] = gap
    for group in range(GROUPS):
        for half in range(2):
            for tile in range(CHUNK_ROWS[group, half] // TILE, SIDE):
                middle[group, half, tile] = jnp.zeros((TILE, PAD), jnp.float32)

    def sideways(source, target, index, device):
        return pltpu.make_async_remote_copy(
            src_ref=source, dst_ref=target, send_sem=side_send.at[index], recv_sem=side_recv.at[index],
            device_id=device, device_id_type=MESH,
        )

    pair_out = [
        sideways(x_ref.at[pl.ds(b * BLOCK, BLOCK)], beside.at[pl.ds(b * PAD, BLOCK)], b, left) for b in range(2)
    ]
    turn_out = sideways(turn.at[0, pl.ds(PAD, PAD)], turn_in, 2, left)
    corner_out = sideways(corner, corner_in, 3, left)
    block_out = sideways(stack.at[PAIRS, pl.ds(0, PAD)], stack.at[0, pl.ds(0, PAD)], 4, right)
    wide_out = sideways(wide, wide_in, 5, right)

    def send(group, half, axis, step, source, target, kind, small=0):
        pltpu.make_async_remote_copy(
            src_ref=source, dst_ref=target, send_sem=send_sem.at[group, half, small],
            recv_sem=recv_sem.at[group, half, kind], device_id=movers[half][axis](step), device_id_type=MESH,
        ).start()

    def arrived(like, group, half, kind):
        pltpu.make_async_copy(like, like, recv_sem.at[group, half, kind]).wait()

    def chunk_of(ref, group, half, step):
        return ref.at[group, half * SIDE + ring(places[half][0], step), pl.ds(0, CHUNK_ROWS[group, half])]

    def slot_of(ref, group, half, slot):
        return ref.at[group, half, slot, pl.ds(0, CHUNK_ROWS[group, half])]

    def slots_of(ref, group, half, count):
        return ref.at[group, half, pl.ds(0, count), pl.ds(0, CHUNK_ROWS[group, half])]

    def spread(group, half):
        send(group, half, 0, 2 * tie, chunk_of(part, group, half, 4), slot_of(relay_in, group, half, 2), 0)
        for slot, step in enumerate((1, -1)):
            send(group, half, 0, step, chunk_of(part, group, half, 3 * step), slot_of(relay_in, group, half, slot), 0)

    def spread_near(group, half):
        for slot, step in enumerate((1, -1)):
            send(group, half, 0, step, chunk_of(part, group, half, step), slot_of(final_in, group, half, slot), 1)

    def relay(group, half):
        arrived(slots_of(relay_in, group, half, 3), group, half, 0)
        for slot, step in enumerate((1, -1)):
            here = chunk_of(part, group, half, 2 * step)[...] + slot_of(relay_in, group, half, slot)[...]
            out = slot_of(relay_out, group, half, slot)
            out[...] = here + jnp.where(tie == step, slot_of(relay_in, group, half, 2)[...], 0.0)
            send(group, half, 0, 2 * step, out, slot_of(final_in, group, half, 2 + slot), 1)

    def met():
        for half in range(2):
            arrived(slots_of(final_in, 0, half, 4), 0, half, 1)

    def cross(group, half):
        if group > 0:
            arrived(slots_of(final_in, group, half, 4), group, half, 1)
        total = chunk_of(part, group, half, 0)[...]
        for slot in range(4):
            total = total + slot_of(final_in, group, half, slot)[...]
        count = CHUNK_ROWS[group, half] // TILE
        middle[group, half, pl.ds(0, count)] = total.reshape(count, TILE, PAD)
        place = places[half][1]
        for step in FAR_FIRST:
            send(
                group, half, 1, step, middle.at[group, half, ring(place, step)], tiles.at[group, half, place], 2, 1
            )
        tiles[group, half, place] = middle[group, half, place]

    def back(group, half):
        arrived(tiles.at[group, half, pl.ds(0, SIDE - 1)], group, half, 2)
        total = tiles[group, half, 0]
        for i in range(1, SIDE):
            total = total + tiles[group, half, i]
        first, second = places[half]
        here = full.at[group, half * SIDE + first, pl.ds(pl.multiple_of(second * TILE, TILE), TILE)]
        here[...] = total
        for step in FAR_FIRST:
            send(group, half, 1, step, here, here, 3, 1)

    def share(group, half):
        arrived(tiles.at[group, half, pl.ds(0, SIDE - 1)], group, half, 3)
        here = chunk_of(full, group, half, 0)
        for step in (2, -2):
            send(group, half, 0, step, here, here, 4)

    def share_near(group, half):
        here = chunk_of(full, group, half, 0)
        for step in (1, -1):
            send(group, half, 0, step, here, here, 5)

    def pass_on(group, half):
        arrived(slots_of(final_in, group, half, 2), group, half, 4)
        here = chunk_of(full, group, half, -2 * tie)
        send(group, half, 0, 2 * tie, here, here, 5)
        for step in (1, -1):
            here = chunk_of(full, group, half, -2 * step)
            send(group, half, 0, step, here, here, 5)

    def complete(group, half):
        arrived(full.at[group, pl.ds(0, 5), pl.ds(0, CHUNK_ROWS[group, half])], group, half, 5)

    def put(group, chunk, x):
        part[group, pl.ds(chunk, 2)] = x[:BLOCK].reshape(2, CHUNK, PAD)

    def take(group, chunk):
        return full[group, pl.ds(chunk, 2), pl.ds(0, CHUNK)].reshape(BLOCK, PAD)

    firsts, lasts, turnings = {}, {}, {}

    def gram_products(half):
        for k in (2 * half, 2 * half + 1):
            for b in range(2 * k + 2 if k else 0, min(2 * k + 4, 2 * PAIRS)):
                loads[b].wait()
            pair = own[k]
            gram = dot_nt(pair, pair)
            put(0, 4 * k, packed(gram[:PAD, :PAD], gram[PAD:, PAD:]))
            between = gram[:BLOCK, PAD:]
            if k < PAIRS - 1:
                kept, extra = folded(dot_nt(pair, own[k + 1]))
                group, half = CROSS_PLACE[k]
                part[group, pl.ds(half * SIDE, SIDE), pl.ds(0, SHORT)] = kept.reshape(SIDE, SHORT, PAD)
                rows = extra.shape[0]
                beginning = jnp.where(lanes(rows) < BLOCK, between[:rows], extra)
                between = jnp.concatenate([beginning, between[rows:]], axis=0)
            put(0, 4 * k + 2, between)

    def begin():
        pl.semaphore_wait(barrier, 2 * len(NEAR) + 2)
        for copy in pair_out:
            copy.start()

    def cross_products(k):
        group, half = CROSS_PLACE[k]
        if k == PAIRS - 1:
            for copy in pair_out:
                copy.wait_recv()
            gram = dot_nt(own[k], beside[...])
            put(group, half * SIDE, gram[:PAD, :PAD])
            put(group, half * SIDE + 2, gram[:PAD, PAD:])
            put(group, half * SIDE + 4, gram[PAD:, :PAD])
            put(group, half * SIDE + 6, gram[PAD:, PAD:])
        spread(group, half)

    def cross_quarters(k):
        group, half = CROSS_PLACE[k]
        if k == PAIRS - 1:
            return [padded(take(group, half * SIDE + 2 * i)) for i in range(4)]
        kept = full[group, pl.ds(half * SIDE, SIDE), pl.ds(0, SHORT)].reshape(SIDE * SHORT, PAD)
        return [padded(x) for x in unfolded(kept, take(0, 4 * k + 2)[: BLOCK - SHORT])]

    def first_turnings(*pairs):
        for k in pairs:
            first, last = unpacked(take(0, 4 * k))
            between = take(0, 4 * k + 2)
            between = padded(jnp.where(lanes(BLOCK) < BLOCK, between, 0.0))
            grams[k] = square_of(first, between, between.T, last)
        for k in pairs:
            turn[k] = turning_transposed(grams[k])
        if 0 in pairs:
            turn_out.start()

    def first_update(k):
        updated = dot(turn[k], own[k]).astype(jnp.bfloat16)
        stack[k + 1, pl.ds(0, PAD)] = updated[:PAD]
        stack[k, pl.ds(PAD, PAD)] = updated[PAD:]

    def turned_grams(*pairs):
        for k in pairs:
            lasts[k] = both_sides(turn[k, pl.ds(PAD, PAD)], grams[k], turn[k, pl.ds(PAD, PAD)])
        if 0 in pairs:
            corner[...] = lasts[0]
            corner_out.start()
        for k in pairs:
            firsts[k] = both_sides(turn[k, pl.ds(0, PAD)], grams[k], turn[k, pl.ds(0, PAD)])
        if PAIRS - 1 in pairs:
            first_update(PAIRS - 1)
            block_out.start()

    def first_updates():
        for k in range(PAIRS - 1):
            first_update(k)

    def update_beside():
        stack[PAIRS, pl.ds(PAD, PAD)] = dot(turn_in[...], beside[...]).astype(jnp.bfloat16)

    def second_turnings(*pairs):
        if PAIRS - 1 in pairs:
            turn_out.wait_recv()
            corner_out.wait_recv()
        between = {}
        for k in pairs:
            cross_gram = square_of(*cross_quarters(k))
            other = turn[k + 1, pl.ds(PAD, PAD)] if k < PAIRS - 1 else turn_in[...]
            between[k] = both_sides(turn[k, pl.ds(0, PAD)], cross_gram, other)
        for k in pairs:
            last = lasts[k + 1] if k < PAIRS - 1 else corner_in[...]
            turnings[k] = turning_transposed(square_of(firsts[k], between[k], between[k].T, last))
        if PAIRS - 1 in pairs:
            wide[...] = turnings[PAIRS - 1][:PAD]
            wide_out.start()
    def second_update(k):
        updated = dot(turnings[k], stack[k + 1]).astype(jnp.bfloat16)
        if k < PAIRS - 1:
            o_ref[pl.ds((2 * k + 1) * BLOCK, BLOCK)] = updated[PAD : PAD + BLOCK]
            o_ref[pl.ds((2 * k + 2) * BLOCK, BLOCK)] = updated[:BLOCK]
        else:
            o_ref[pl.ds((2 * k + 1) * BLOCK, BLOCK)] = jnp.where(c == col_count - 1, stack[PAIRS, pl.ds(0, BLOCK)], updated[PAD : PAD + BLOCK])

    def first_block():
        block_out.wait_recv()
        wide_out.wait_recv()
        updated = dot(wide_in[...], stack[0]).astype(jnp.bfloat16)[:BLOCK]
        o_ref[pl.ds(0, BLOCK)] = jnp.where(c == 0, stack[0, pl.ds(PAD, BLOCK)], updated)

    plan = [(0, gram_products, 0), (0, begin), (0, spread, 0, 0), (0, gram_products, 1), (0, spread, 0, 1)]
    plan += [(LAG, cross_products, k) for k in (0, 1, 3, 2)]
    units = [(0, 0), (0, 1)] + [CROSS_PLACE[k] for k in CROSS_ORDER]
    for i, unit in enumerate(units):
        for j, stage in enumerate((relay, cross, back, share, pass_on, complete)):
            plan.append(((j + 1) * STAGE + (LAG if i >= 2 else 0), stage, *unit))
    plan.append((54.9, complete, 0, 0))
    plan.append((54.9, first_turnings, 0))
    plan.append((54.9, turned_grams, 0))
    plan += [(LAG + 0.5, spread_near, *unit) for unit in units]
    plan += [(4 * STAGE + LAG + 0.5, share_near, *unit) for unit in units]
    plan.append((2 * STAGE - 0.01, met))
    plan.append((TURN, first_turnings, 1, 2, 3))
    plan.append((TURN, turned_grams, 1, 2, 3))
    plan.append((64.5, complete, *CROSS_PLACE[3]))
    plan.append((64.5, second_turnings, 3))
    plan.append((100, second_turnings, 0, 1, 2))
    plan.append((100, first_updates))
    plan.append((100, update_beside))
    plan += [(100, second_update, k) for k in range(PAIRS)]
    plan.append((100, first_block))
    plan.remove((6 * STAGE, complete, 0, 0))
    plan.remove((6 * STAGE + LAG, complete, *CROSS_PLACE[3]))
    for _, step, *where in sorted(plan, key=lambda entry: entry[0]):
        step(*where)

    for copy in pair_out + [turn_out, corner_out, block_out, wide_out]:
        copy.wait_send()
    for group in range(GROUPS):
        for half in range(2):
            for small, like in enumerate((full.at[group, pl.ds(0, 14), pl.ds(0, CHUNK_ROWS[group, half])], part.at[group, pl.ds(0, 2)])):
                pltpu.make_async_copy(like, like, send_sem.at[group, half, small]).wait()


def shards(weight_delta):
    width = weight_delta.shape[1]
    chunks = lambda count: pltpu.VMEM((GROUPS, 2, count, CHUNK, PAD), f32)
    f32, bf16 = jnp.float32, jnp.bfloat16
    return pl.pallas_call(
        kernel,
        out_shape=pltpu.VMEM(weight_delta.shape, bf16),
        in_specs=[pl.BlockSpec(memory_space=pl.ANY)],
        out_specs=pl.BlockSpec(memory_space=pltpu.VMEM),
        scratch_shapes=[
            pltpu.VMEM((PAIRS, 2 * PAD, width), bf16),
            pltpu.VMEM((2 * PAD, width), bf16),
            pltpu.VMEM((GROUPS, 2 * SIDE, CHUNK, PAD), f32),
            chunks(3),
            chunks(2),
            chunks(4),
            pltpu.VMEM((GROUPS, 2, SIDE, TILE, PAD), f32),
            pltpu.VMEM((GROUPS, 2, SIDE, TILE, PAD), f32),
            pltpu.VMEM((GROUPS, 2 * SIDE, SIDE * TILE, PAD), f32),
            pltpu.VMEM((PAIRS, 2 * PAD, 2 * PAD), f32),
            pltpu.VMEM((PAIRS, 2 * PAD, 2 * PAD), bf16),
            pltpu.VMEM((PAIRS + 1, 2 * PAD, width), bf16),
            pltpu.VMEM((PAD, PAD), f32),
            pltpu.VMEM((PAD, PAD), f32),
            pltpu.VMEM((PAD, 2 * PAD), bf16),
            pltpu.VMEM((PAD, 2 * PAD), bf16),
            pltpu.VMEM((PAD, 2 * PAD), bf16),
            pltpu.SemaphoreType.DMA((2 * PAIRS,)),
            pltpu.SemaphoreType.DMA((GROUPS, 2, 2)),
            pltpu.SemaphoreType.DMA((GROUPS, 2, 6)),
            pltpu.SemaphoreType.DMA((6,)),
            pltpu.SemaphoreType.DMA((6,)),
        ],
        compiler_params=pltpu.CompilerParams(
            collective_id=0, has_side_effects=True, vmem_limit_bytes=58 * 2**20
        ),
    )(weight_delta)


def solution(mesh):
    return jax.shard_map(
        shards, mesh=mesh, in_specs=(P("col", "row"),), out_specs=P("col", "row"), check_vma=False
    )
```
